32 devices in a mesh: dp: 16 (over z, y, core), rep: 2 (over x).
Axes of the slice: x: 2, y: 2, z: 4, core: 2. Of those that a mesh axis runs over, the one named last changes fastest.
Arguments:
- features: bfloat16 [4096, 1152], P('dp'), may hold values from -0.046875 to 0.046875
- img_weight: bfloat16 [1152, 1152], P(None, 'rep'), may hold values from -4 to 4
- text_embed: bfloat16 [4096, 1152], P('dp', 'rep'), may hold values from -0.4375 to 0.4375
- log_scale: float32 [1], replicated, may hold values from 1.6 to 2.6
- logit_bias: float32 [1], replicated, may hold values from -4 to -1
Outputs:
- image_grad: bfloat16 [4096, 1152], P('dp', 'rep')
- text_grad: bfloat16 [4096, 1152], P('dp', 'rep')
- weight_grad: bfloat16 [1152, 1152], P(None, 'rep')
The draws below stay inside these ranges and needn't reach their ends.
All inputs are finite; a program needn't handle non-finite values.
Results may differ from the reference program's by a relative error of at most 0.017.
Values may be sent and summed in bfloat16 or wider, within the bound.
A program may use at most 64 MiB of HBM per device.

```python
import jax
import jax.numpy as jnp
from jax import lax

D = 1152
E = 1152
TOK_DEV = 256
STEPS = 4
TOKENS = 4096
N_DP = 16


def shard_levels(stream_key, extent, split, least, largest):
    def one(position, blocks):
        heights = jax.random.uniform(jax.random.fold_in(jax.random.fold_in(stream_key, 6), position), (blocks,), jnp.float32, least / len(split), largest / len(split))
        return jnp.repeat(jnp.exp(heights), extent[position] // blocks).reshape((-1,) + (1,) * (len(extent) - position - 1))

    loudness = one(*split[0])
    for cut in split[1:]:
        loudness = loudness * one(*cut)
    return loudness


def noise(key, dims, width, most, shards=(), held_as=jnp.bfloat16):
    values = width * jax.random.normal(key, dims, jnp.float32)
    if shards:
        values = values * shard_levels(key, dims, shards, -0.22, 0.18)
    return jnp.clip(values, -most, most).astype(held_as)


def setup_inputs(seed: int = 0) -> dict:
    splits = jax.random.split(jax.random.key(seed), 6)
    return {
        "features": noise(splits[0], (TOKENS, D), 0.003, 0.046875, ((0, 16),)),
        "img_weight": noise(splits[1], (D, E), 0.3, 4.0, ((1, 2),)),
        "text_embed": noise(splits[2], (TOKENS, E), 0.03, 0.4375, ((0, 16), (1, 2))),
        "log_scale": jnp.clip(jax.random.uniform(splits[3], (1,), jnp.float32, 1.6, 2.6), 1.6, 2.6),
        "logit_bias": jnp.clip(jax.random.uniform(splits[4], (1,), jnp.float32, -4.0, -1.0), -4.0, -1.0),
    }


epsilon = 1e-06

def reference(features, img_weight, text_embed, log_scale, logit_bias):
    logit_scale = jnp.exp(log_scale[0])
    offset_value = logit_bias[0]
    img_raw = jnp.dot(features, img_weight, preferred_element_type=jnp.float32)
    img_inv = lax.rsqrt(lax.optimization_barrier(jnp.sum(img_raw * img_raw, axis=1, keepdims=True)) + epsilon)
    img_hat = img_raw * img_inv
    txt_raw = text_embed.astype(jnp.float32)
    txt_inv = lax.rsqrt(lax.optimization_barrier(jnp.sum(txt_raw * txt_raw, axis=1, keepdims=True)) + epsilon)
    txt_hat = txt_raw * txt_inv
    img_blocks = lax.optimization_barrier(img_hat.astype(jnp.bfloat16)).astype(jnp.float32).reshape(N_DP, TOK_DEV, E)
    txt_blocks = lax.optimization_barrier(txt_hat.astype(jnp.bfloat16)).astype(jnp.float32).reshape(N_DP, TOK_DEV, E)
    positives = jnp.eye(TOK_DEV, dtype=jnp.float32)
    grad_img = jnp.zeros((N_DP, TOK_DEV, E), jnp.float32)
    grad_txt = jnp.zeros((N_DP, TOK_DEV, E), jnp.float32)
    for stride in range(STEPS + 1):
        text_span = jnp.roll(txt_blocks, stride, axis=0)
        logits = logit_scale * jnp.einsum('kie,kje->kij', img_blocks, text_span) + offset_value
        sig_grad = jax.nn.sigmoid(logits)
        if stride == 0:
            sig_grad = sig_grad - positives
        grad_bf = lax.optimization_barrier(sig_grad.astype(jnp.bfloat16)).astype(jnp.float32)
        grad_img = grad_img + logit_scale * jnp.einsum('kij,kje->kie', grad_bf, text_span)
        contrib = logit_scale * jnp.einsum('kij,kie->kje', grad_bf, img_blocks)
        grad_txt = grad_txt + jnp.roll(contrib, -stride, axis=0)
    grad_img = grad_img.reshape(TOKENS, E)
    grad_txt = grad_txt.reshape(TOKENS, E)
    img_dot = lax.optimization_barrier(jnp.sum(img_hat * grad_img, axis=1, keepdims=True))
    txt_dot = lax.optimization_barrier(jnp.sum(txt_hat * grad_txt, axis=1, keepdims=True))
    image_grad = ((grad_img - img_hat * img_dot) * img_inv).astype(jnp.bfloat16)
    text_grad = ((grad_txt - txt_hat * txt_dot) * txt_inv).astype(jnp.bfloat16)
    weight_grad = jnp.dot(features.T, image_grad, preferred_element_type=jnp.float32).astype(jnp.bfloat16)
    return (image_grad, text_grad, weight_grad)
```

```python
import functools

import jax
import jax.numpy as jnp
from jax import lax
from jax.experimental import pallas as pl
from jax.experimental.pallas import tpu as pltpu
from jax.sharding import PartitionSpec as P

STEPS = 4
EPSILON = 1e-06
F32 = jnp.float32
BF16 = jnp.bfloat16
MESH = pl.DeviceIdType.MESH


def to_rows(first, second):
    n = first.shape[0]
    lane = lax.broadcasted_iota(jnp.int32, (n, 128), 1)
    return jnp.transpose(jnp.where(lane == 0, first, second))[:8]


def to_columns(rows):
    n = rows.shape[1]
    return jnp.transpose(jnp.concatenate([rows, jnp.zeros((120, n), F32)], axis=0))


def kernel(
    n, features, weight, text, log_scale, bias, img_out, txt_out, w_out,
    img_hat, img_bf, img_inv, txt_hat, txt_inv, span, d_img, d_txt, dots,
    own_score, score_out, score_in, back, from_core, sum_two, sum_four, two_in, four_in,
    feat_t, acc, half_out, half_in, quarter_out, quarter_in, eighth_out, eighth_in,
    last_out, last_in, rows_out, rows_in,
    s_span, r_span, s_score, r_score, s_back, r_back, s_w, r_w, s_rows, r_rows,
):
    k = lax.axis_index("dp")
    x = lax.axis_index("rep")
    tok = features.shape[0]
    part = weight.shape[1]
    odd = lax.rem(k, 2)
    high = lax.rem(k // 2, 2)

    def bit(b):
        return lax.rem(k // b, 2)

    def flip(b):
        return k + b - 2 * b * bit(b)

    def at(offset):
        return (lax.rem(k + offset + n, n), x)

    core = (flip(1), x)
    across = (k, 1 - x)
    far = []
    b = 8
    while b < n:
        far.append(b)
        b *= 2

    def copy(src, dst, s, r, device):
        return pltpu.make_async_remote_copy(
            src_ref=src, dst_ref=dst, send_sem=s, recv_sem=r,
            device_id=device, device_id_type=MESH,
        )

    barrier = pltpu.get_barrier_semaphore()
    friends = [across, core, at(2), at(-2), at(4), at(-4)] + [(flip(b), x) for b in far]
    for friend in friends:
        pl.semaphore_signal(barrier, inc=1, device_id=friend, device_id_type=MESH)

    raw = jnp.dot(features[...], weight[...], preferred_element_type=F32)
    txt_raw = text[...].astype(F32)
    sums = to_rows(
        jnp.sum(raw * raw, axis=1, keepdims=True),
        jnp.sum(txt_raw * txt_raw, axis=1, keepdims=True),
    )
    rows_out[0] = sums
    img_hat[...] = raw
    pl.semaphore_wait(barrier, len(friends))

    c = copy(rows_out.at[0], rows_in.at[0], s_rows.at[0], r_rows.at[0], across)
    c.start()
    feat_t[...] = jnp.transpose(features[...])
    c.wait()
    inverse = lax.rsqrt(to_columns(sums + rows_in[0]) + EPSILON)
    img_inv[...] = inverse[:, 0:1]
    txt_inv[...] = inverse[:, 1:2]
    hat = text[...].astype(F32) * txt_inv[...]
    txt_hat[...] = hat
    span[0] = hat.astype(BF16)

    own_four = copy(span.at[0], span.at[4], s_span.at[0], r_span.at[4], at(4))
    own_two = copy(span.at[0], span.at[2], s_span.at[1], r_span.at[2], at(2))
    pass_two = copy(span.at[4], span.at[2], s_span.at[1], r_span.at[2], at(-2))
    own_one = copy(span.at[0], span.at[1], s_span.at[2], r_span.at[1], core)
    pass_four = copy(span.at[4], span.at[3], s_span.at[2], r_span.at[3], core)
    slot = 3 - 2 * odd
    share_two = copy(span.at[2], span.at[slot], s_span.at[3], r_span.at[slot], core)

    own_four.start()

    @pl.when(high == 0)
    def _():
        own_two.start()

    @pl.when(odd == 0)
    def _():
        own_one.start()

    hat = img_hat[...] * img_inv[...]
    img_hat[...] = hat
    img_bf[...] = hat.astype(BF16)
    t_wide = jnp.exp(jnp.full((1, tok), log_scale[0], F32))
    t_part = jnp.exp(jnp.full((1, part), log_scale[0], F32))

    def arrived(s):
        copy(span.at[s], span.at[s], s_span.at[0], r_span.at[s], core).wait_recv()

    def score_copy(s):
        return copy(score_out.at[s], score_in.at[s], s_score.at[s], r_score.at[s], across)

    def begin(s):
        score = lax.dot_general(
            img_bf[...], span[s], (((1,), (1,)), ((), ())), preferred_element_type=F32
        )
        own_score[s] = score
        score_out[s] = score.astype(BF16)
        score_copy(s).start()

    def finish(s, first=False):
        score_copy(s).wait()
        score = own_score[s] + score_in[s].astype(F32)
        g = jax.nn.sigmoid(t_wide * score + bias[0])
        if s == 0:
            row = lax.broadcasted_iota(jnp.int32, (tok, tok), 0)
            col = lax.broadcasted_iota(jnp.int32, (tok, tok), 1)
            g = g - jnp.where(row == col, 1.0, 0.0)
        g = g.astype(BF16)
        dot = jnp.sum(g.astype(F32) * score, axis=1, keepdims=True)
        term = jnp.dot(g, span[s], preferred_element_type=F32)
        if first:
            d_img[...] = term
            dots[...] = dot
        else:
            d_img[...] += term
            dots[...] += dot
        return g

    def returned(g):
        return lax.dot_general(
            g, img_bf[...], (((0,), (0,)), ((), ())), preferred_element_type=F32
        )

    def core_copy(i):
        return copy(back.at[2 * i], from_core.at[i], s_back.at[i], r_back.at[i], core)

    begin(0)
    arrived(4)

    @pl.when(high == 1)
    def _():
        pass_two.start()

    @pl.when(odd == 1)
    def _():
        pass_four.start()

    begin(4)
    d_txt[...] = returned(finish(0, True))
    arrived(2)
    share_two.start()
    begin(2)
    back[3] = returned(finish(4)).astype(BF16)
    arrived(3)
    begin(3)
    back[1] = returned(finish(2)).astype(BF16)
    arrived(1)
    begin(1)
    back[2] = returned(finish(3)).astype(BF16)
    core_copy(1).start()
    g = finish(1)
    back[0] = returned(g).astype(BF16)
    core_copy(0).start()

    grad = ((d_img[...] - img_hat[...] * dots[...]) * t_part * img_inv[...]).astype(BF16)
    img_out[...] = grad

    depth = feat_t.shape[0]
    half, quarter, eighth = depth // 2, depth // 4, depth // 8

    def rows(start, size):
        return pl.ds(pl.multiple_of(start, 16), size)

    half_out[...] = jnp.dot(
        feat_t[rows((1 - odd) * half, half), :], img_out[...], preferred_element_type=F32
    ).astype(BF16)
    one = copy(half_out, half_in, s_w.at[0], r_w.at[0], core)
    one.start()
    acc[...] = jnp.dot(feat_t[rows(odd * half, half), :], img_out[...], preferred_element_type=F32)

    core_copy(0).wait_recv()
    core_copy(1).wait_recv()
    oddf = odd.astype(F32)
    highf = high.astype(F32)
    sum_two[...] = (back[1].astype(F32) + from_core[1 - odd].astype(F32)).astype(BF16)
    send_two = copy(sum_two, two_in, s_back.at[2], r_back.at[2], (flip(2), x))
    send_four = copy(sum_four, four_in, s_back.at[3], r_back.at[3], at(-4))

    first_b, second_b = 2 + 2 * odd, 4 - 2 * odd
    first_bit = high * (1 - odd) + bit(4) * odd
    second_bit = high * odd + bit(4) * (1 - odd)
    first_peer = (k + first_b - 2 * first_b * first_bit, x)
    second_peer = (k + second_b - 2 * second_b * second_bit, x)

    one.wait()
    acc[...] += half_in[...].astype(F32)
    quarter_out[...] = acc[rows((1 - first_bit) * quarter, quarter), :].astype(BF16)
    two = copy(quarter_out, quarter_in, s_w.at[1], r_w.at[1], first_peer)
    two.start()
    send_two.start()

    @pl.when(high == 0)
    def _():
        sum_four[...] = (back[3].astype(F32) + from_core[1].astype(F32) * oddf).astype(BF16)
        send_four.start()

    two.wait()
    keep = first_bit * quarter
    acc[rows(keep, quarter), :] += quarter_in[...].astype(F32)
    eighth_out[...] = acc[rows(keep + (1 - second_bit) * eighth, eighth), :].astype(BF16)
    three = copy(eighth_out, eighth_in, s_w.at[2], r_w.at[2], second_peer)
    three.start()

    send_two.wait()

    @pl.when(high == 1)
    def _():
        sum_four[...] = (
            back[3].astype(F32) + from_core[1].astype(F32) * oddf + two_in[...].astype(F32)
        ).astype(BF16)
        send_four.start()

    three.wait()
    keep = keep + second_bit * eighth
    total = acc[rows(keep, eighth), :] + eighth_in[...].astype(F32)
    for i, b in enumerate(far):
        last_out[i] = total.astype(BF16)
        c = copy(last_out.at[i], last_in.at[i], s_w.at[6 + i], r_w.at[6 + i], (flip(b), x))
        c.start()
        c.wait()
        total = last_out[i].astype(F32) + last_in[i].astype(F32)
    mine = odd * half + keep
    w_out[rows(mine, eighth), :] = total.astype(BF16)

    def spread(i, start, size, device):
        piece = w_out.at[rows(start, size), :]
        return copy(piece, piece, s_w.at[i], r_w.at[i], device)

    def landed(i, start, size):
        piece = w_out.at[rows(start, size), :]
        copy(piece, piece, s_w.at[i], r_w.at[i], core).wait_recv()

    c3 = spread(3, mine, eighth, second_peer)
    c3.start()

    send_four.wait()
    even = 1.0 - oddf
    grad = (
        d_txt[...] + four_in[...].astype(F32) + from_core[0].astype(F32) * even
        + two_in[...].astype(F32) * (1.0 - highf)
    )
    d_txt[...] = grad
    dot = jnp.sum(txt_hat[...] * grad, axis=1, keepdims=True)
    sums = to_rows(dot, dot)
    rows_out[1] = sums
    cd = copy(rows_out.at[1], rows_in.at[1], s_rows.at[1], r_rows.at[1], across)
    cd.start()

    quarter_at = odd * half + first_bit * quarter
    landed(3, quarter_at + (1 - second_bit) * eighth, eighth)
    c4 = spread(4, quarter_at, quarter, first_peer)
    c4.start()

    cd.wait()
    dot = to_columns(sums + rows_in[1])[:, 0:1]
    txt_out[...] = ((d_txt[...] - txt_hat[...] * dot) * t_part * txt_inv[...]).astype(BF16)

    landed(4, odd * half + (1 - first_bit) * quarter, quarter)
    c5 = spread(5, odd * half, half, core)
    c5.start()
    landed(5, (1 - odd) * half, half)

    c3.wait_send()
    c4.wait_send()
    c5.wait_send()
    own_four.wait_send()
    share_two.wait_send()
    core_copy(0).wait_send()
    core_copy(1).wait_send()

    @pl.when(high == 0)
    def _():
        own_two.wait_send()

    @pl.when(high == 1)
    def _():
        pass_two.wait_send()

    @pl.when(odd == 0)
    def _():
        own_one.wait_send()

    @pl.when(odd == 1)
    def _():
        pass_four.wait_send()


def shards(n, features, img_weight, text_embed, log_scale, logit_bias):
    tok, depth = features.shape
    part = img_weight.shape[1]
    vmem = pl.BlockSpec(memory_space=pltpu.VMEM)
    smem = pl.BlockSpec(memory_space=pltpu.SMEM)
    block = lambda dtype, *lead: pltpu.VMEM((*lead, tok, part), dtype)
    levels = 0
    while 8 << levels < n:
        levels += 1
    dma = pltpu.SemaphoreType.DMA
    pairs = STEPS + 1
    return pl.pallas_call(
        functools.partial(kernel, n),
        out_shape=(
            jax.ShapeDtypeStruct((tok, part), BF16),
            jax.ShapeDtypeStruct((tok, part), BF16),
            jax.ShapeDtypeStruct((depth, part), BF16),
        ),
        in_specs=[vmem, vmem, vmem, smem, smem],
        out_specs=(vmem, vmem, vmem),
        scratch_shapes=[
            block(F32), block(BF16), pltpu.VMEM((tok, 1), F32),
            block(F32), pltpu.VMEM((tok, 1), F32),
            block(BF16, pairs), block(F32), block(F32), pltpu.VMEM((tok, 1), F32),
            pltpu.VMEM((pairs, tok, tok), F32),
            pltpu.VMEM((pairs, tok, tok), BF16), pltpu.VMEM((pairs, tok, tok), BF16),
            block(BF16, 4), block(BF16, 2), block(BF16), block(BF16), block(BF16), block(BF16),
            pltpu.VMEM((depth, tok), BF16), pltpu.VMEM((depth // 2, part), F32),
            pltpu.VMEM((depth // 2, part), BF16), pltpu.VMEM((depth // 2, part), BF16),
            pltpu.VMEM((depth // 4, part), BF16), pltpu.VMEM((depth // 4, part), BF16),
            pltpu.VMEM((depth // 8, part), BF16), pltpu.VMEM((depth // 8, part), BF16),
            pltpu.VMEM((max(levels, 1), depth // 8, part), BF16),
            pltpu.VMEM((max(levels, 1), depth // 8, part), BF16),
            pltpu.VMEM((2, 8, tok), F32), pltpu.VMEM((2, 8, tok), F32),
            dma((4,)), dma((pairs,)), dma((pairs,)), dma((pairs,)), dma((4,)), dma((4,)),
            dma((6 + max(levels, 1),)), dma((6 + max(levels, 1),)), dma((2,)), dma((2,)),
        ],
        compiler_params=pltpu.CompilerParams(
            collective_id=0, has_side_effects=True, vmem_limit_bytes=48 * 1024 * 1024
        ),
    )(features, img_weight, text_embed, log_scale, logit_bias)


def solution(mesh):
    in_specs = (P("dp", None), P(None, "rep"), P("dp", "rep"), P(), P())
    out_specs = (P("dp", "rep"), P("dp", "rep"), P(None, "rep"))
    body = functools.partial(shards, mesh.shape["dp"])
    return jax.shard_map(body, mesh=mesh, in_specs=in_specs, out_specs=out_specs, check_vma=False)
```

```python
import functools

import jax
import jax.numpy as jnp
from jax import lax
from jax.experimental import pallas as pl
from jax.experimental.pallas import tpu as pltpu
from jax.sharding import PartitionSpec as P

STEPS = 4
CHUNKS = 2
TAIL = 16
EPSILON = 1e-06
F32 = jnp.float32
BF16 = jnp.bfloat16
MESH = pl.DeviceIdType.MESH


def kernel(
    n, features, weight, text, log_scale, bias, img_out, txt_out, w_out,
    img_hat, img_bf, img_rows, img_inv, span, squares, inverses, d_img, d_txt, dots,
    own_score, score_out, score_in, back, from_core, sum_two, sum_four, two_in, four_in,
    acc, half_out, half_in, quarter_out, quarter_in, eighth_out, eighth_in,
    last_out, last_in, rows_out, rows_in,
    s_span, r_span, s_score, r_score, s_back, r_back, s_w, r_w, s_rows, r_rows,
):
    k = lax.axis_index("dp")
    x = lax.axis_index("rep")
    tok = features.shape[0]
    part = weight.shape[0]
    odd = lax.rem(k, 2)
    high = lax.rem(k // 2, 2)

    def bit(b):
        return lax.rem(k // b, 2)

    def flip(b):
        return k + b - 2 * b * bit(b)

    def at(offset):
        return (lax.rem(k + offset + n, n), x)

    core = (flip(1), x)
    across = (k, 1 - x)
    far = []
    b = 8
    while b < n:
        far.append(b)
        b *= 2

    def copy(src, dst, s, r, device):
        return pltpu.make_async_remote_copy(
            src_ref=src, dst_ref=dst, send_sem=s, recv_sem=r,
            device_id=device, device_id_type=MESH,
        )

    barrier = pltpu.get_barrier_semaphore()
    friends = [across, core, at(2), at(-2), at(4), at(-4)] + [(flip(b), x) for b in far]
    for friend in friends:
        pl.semaphore_signal(barrier, inc=1, device_id=friend, device_id_type=MESH)
    pl.semaphore_wait(barrier, len(friends))

    size = part // CHUNKS

    def text_copy(source, target, c, device, i):
        piece = pl.ds(c * size, size)
        src = text if source is None else span.at[source]
        return copy(
            src.at[piece], span.at[target, piece], s_span.at[i, c], r_span.at[target, c], device
        )

    def arrived(s, c):
        piece = pl.ds(c * size, size)
        copy(
            span.at[s, piece], span.at[s, piece], s_span.at[0, c], r_span.at[s, c], core
        ).wait_recv()

    slot = 3 - 2 * odd
    own_four = [text_copy(None, 4, c, at(4), 0) for c in range(CHUNKS)]
    own_two = [text_copy(None, 2, c, at(2), 1) for c in range(CHUNKS)]
    pass_two = [text_copy(4, 2, c, at(-2), 1) for c in range(CHUNKS)]
    own_one = [text_copy(None, 1, c, core, 2) for c in range(CHUNKS)]
    pass_four = [text_copy(4, 3, c, core, 2) for c in range(CHUNKS)]
    share_two = [text_copy(2, slot, c, core, 3) for c in range(CHUNKS)]

    for c in range(CHUNKS):
        own_four[c].start()

        @pl.when(high == 0)
        def _():
            own_two[c].start()

        @pl.when(odd == 0)
        def _():
            own_one[c].start()

    def along(a, b):
        return lax.dot_general(a, b, (((1,), (1,)), ((), ())), preferred_element_type=F32)

    raw = along(weight[...], features[...])
    img_hat[...] = raw
    mine = jnp.sum(raw * raw, axis=0, keepdims=True)
    rows_out[0] = jnp.broadcast_to(mine, (8, tok))
    c = copy(rows_out.at[0], rows_in.at[0], s_rows.at[0], r_rows.at[0], across)
    c.start()
    t_wide = jnp.exp(jnp.full((1, tok), log_scale[0], F32))
    c.wait()
    inverse = lax.rsqrt(mine + rows_in[0, 0:1, :] + EPSILON)
    img_inv[...] = jnp.broadcast_to(inverse, (8, tok))
    hat = img_hat[...] * inverse
    img_hat[...] = hat
    img_bf[...] = hat.astype(BF16)
    img_rows[...] = jnp.transpose(img_bf[...])

    def text_of(s):
        return text[...] if s == 0 else span[s]

    def score_copy(s):
        return copy(score_out.at[s], score_in.at[s], s_score.at[s], r_score.at[s], across)

    def begin(s):
        block = text_of(s)
        score = jnp.dot(img_rows[...], block, preferred_element_type=F32)
        own_score[s] = score
        score_out[s, 0:tok, :] = score.astype(BF16)
        wide = block.astype(F32)
        square = jnp.sum(wide * wide, axis=0, keepdims=True)
        squares[s] = jnp.broadcast_to(square, (8, tok))
        top = square.astype(BF16).astype(F32)
        middle = (square - top).astype(BF16).astype(F32)
        low = square - top - middle
        row = lax.broadcasted_iota(jnp.int32, (TAIL, tok), 0)
        tail = jnp.where(row == 0, top, jnp.where(row == 1, middle, low))
        score_out[s, tok : tok + TAIL, :] = tail.astype(BF16)
        score_copy(s).start()

    def finish(s, first=False):
        score_copy(s).wait()
        tail = score_in[s, tok : tok + TAIL, :].astype(F32)
        square = squares[s, 0:1, :] + (tail[0:1] + tail[1:2] + tail[2:3])
        inverse = lax.rsqrt(square + EPSILON)
        if s == 0:
            inverses[...] = jnp.broadcast_to(inverse, (8, tok))
        score = (own_score[s] + score_in[s, 0:tok, :].astype(F32)) * inverse
        g = jax.nn.sigmoid(t_wide * score + bias[0])
        if s == 0:
            row = lax.broadcasted_iota(jnp.int32, (tok, tok), 0)
            col = lax.broadcasted_iota(jnp.int32, (tok, tok), 1)
            g = g - jnp.where(row == col, 1.0, 0.0)
        term = along(text_of(s), (g * inverse).astype(BF16))
        if first:
            d_img[...] = term
            dots[...] = g * score
        else:
            d_img[...] += term
            dots[...] += g * score
        return g.astype(BF16)

    def returned(g):
        return jnp.dot(img_bf[...], g, preferred_element_type=F32)

    def core_copy(i):
        return copy(back.at[2 * i], from_core.at[i], s_back.at[i], r_back.at[i], core)

    begin(0)
    for c in range(CHUNKS):
        arrived(4, c)

        @pl.when(high == 1)
        def _():
            pass_two[c].start()

        @pl.when(odd == 1)
        def _():
            pass_four[c].start()

    begin(4)
    d_txt[...] = returned(finish(0, True))
    for c in range(CHUNKS):
        arrived(2, c)
        share_two[c].start()
    begin(2)
    back[3] = returned(finish(4)).astype(BF16)
    for c in range(CHUNKS):
        arrived(3, c)
    begin(3)
    back[1] = returned(finish(2)).astype(BF16)
    for c in range(CHUNKS):
        arrived(1, c)
    begin(1)
    back[2] = returned(finish(3)).astype(BF16)
    core_copy(1).start()
    last_g = finish(1)

    dot = jnp.sum(jnp.transpose(dots[...]), axis=0, keepdims=True)
    grad = (d_img[...] - img_hat[...] * dot) * (t_wide * img_inv[0:1, :])
    img_out[...] = grad.astype(BF16)

    half, quarter = part // 2, part // 4
    eighth = (quarter // 2 + 15) // 16 * 16
    rest = quarter - eighth

    def rows(start, size):
        return pl.ds(pl.multiple_of(start, 16), size)

    half_out[...] = jnp.dot(
        img_out[rows((1 - odd) * half, half), :], features[...], preferred_element_type=F32
    ).astype(BF16)
    one = copy(half_out, half_in, s_w.at[0], r_w.at[0], core)
    one.start()
    back[0] = returned(last_g).astype(BF16)
    core_copy(0).start()
    acc[...] = jnp.dot(img_out[rows(odd * half, half), :], features[...], preferred_element_type=F32)

    oddf = odd.astype(F32)
    highf = high.astype(F32)
    send_two = copy(sum_two, two_in, s_back.at[2], r_back.at[2], (flip(2), x))
    send_four = copy(sum_four, four_in, s_back.at[3], r_back.at[3], at(-4))

    first_b, second_b = 2 + 2 * odd, 4 - 2 * odd
    first_bit = high * (1 - odd) + bit(4) * odd
    second_bit = high * odd + bit(4) * (1 - odd)
    first_peer = (k + first_b - 2 * first_b * first_bit, x)
    second_peer = (k + second_b - 2 * second_b * second_bit, x)

    one.wait()
    acc[...] += half_in[...].astype(F32)
    quarter_out[...] = acc[rows((1 - first_bit) * quarter, quarter), :].astype(BF16)
    two = copy(quarter_out, quarter_in, s_w.at[1], r_w.at[1], first_peer)
    two.start()

    core_copy(0).wait_recv()
    core_copy(1).wait_recv()
    sum_two[...] = (back[1].astype(F32) + from_core[1 - odd].astype(F32)).astype(BF16)

    two.wait()
    keep = first_bit * quarter
    acc[rows(keep, quarter), :] += quarter_in[...].astype(F32)
    eighth_out[...] = acc[rows(keep + (1 - second_bit) * rest, eighth), :].astype(BF16)
    three = copy(eighth_out, eighth_in, s_w.at[2], r_w.at[2], second_peer)
    three.start()
    three.wait()
    total = acc[rows(keep + second_bit * rest, eighth), :] + eighth_in[...].astype(F32)
    for i, b in enumerate(far):
        last_out[i] = total.astype(BF16)
        c = copy(last_out.at[i], last_in.at[i], s_w.at[6 + i], r_w.at[6 + i], (flip(b), x))
        c.start()
        if i == 0:
            send_two.start()
        c.wait()
        total = last_out[i].astype(F32) + last_in[i].astype(F32)
    last_out[0] = total.astype(BF16)
    base = odd * half + keep

    def spread(i, start, size, device):
        piece = w_out.at[rows(start, size), :]
        return copy(piece, piece, s_w.at[i], r_w.at[i], device)

    def landed(i, start, size):
        piece = w_out.at[rows(start, size), :]
        copy(piece, piece, s_w.at[i], r_w.at[i], core).wait_recv()

    @pl.when(second_bit == 0)
    def _():
        w_out[rows(base, eighth), :] = last_out[0]
        spread(3, base, eighth, second_peer).start()

    @pl.when(second_bit == 1)
    def _():
        w_out[rows(base + eighth, rest), :] = last_out[0, eighth - rest :, :]
        spread(3, base + eighth, rest, second_peer).start()

    @pl.when(high == 0)
    def _():
        sum_four[...] = (back[3].astype(F32) + from_core[1].astype(F32) * oddf).astype(BF16)
        send_four.start()

    @pl.when(second_bit == 0)
    def _():
        spread(3, base, eighth, second_peer).wait_send()
        landed(3, base + eighth, rest)

    @pl.when(second_bit == 1)
    def _():
        spread(3, base + eighth, rest, second_peer).wait_send()
        landed(3, base, eighth)

    c4 = spread(4, base, quarter, first_peer)
    c4.start()

    send_two.wait()

    @pl.when(high == 1)
    def _():
        sum_four[...] = (
            back[3].astype(F32) + from_core[1].astype(F32) * oddf + two_in[...].astype(F32)
        ).astype(BF16)
        send_four.start()

    landed(4, odd * half + (1 - first_bit) * quarter, quarter)
    c5 = spread(5, odd * half, half, core)
    c5.start()

    send_four.wait()
    even = 1.0 - oddf
    grad = (
        d_txt[...] + four_in[...].astype(F32) + from_core[0].astype(F32) * even
        + two_in[...].astype(F32) * (1.0 - highf)
    )
    d_txt[...] = grad
    hat = text[...].astype(F32) * inverses[0:1, :]
    dot = jnp.sum(hat * grad, axis=0, keepdims=True)
    rows_out[1] = jnp.broadcast_to(dot, (8, tok))
    cd = copy(rows_out.at[1], rows_in.at[1], s_rows.at[1], r_rows.at[1], across)
    cd.start()
    cd.wait()
    dot = dot + rows_in[1, 0:1, :]
    inverse = inverses[0:1, :]
    hat = text[...].astype(F32) * inverse
    txt_out[...] = ((d_txt[...] - hat * dot) * (t_wide * inverse)).astype(BF16)

    landed(5, (1 - odd) * half, half)
    c4.wait_send()
    c5.wait_send()
    core_copy(0).wait_send()
    core_copy(1).wait_send()
    for c in range(CHUNKS):
        own_four[c].wait_send()
        share_two[c].wait_send()

        @pl.when(high == 0)
        def _():
            own_two[c].wait_send()

        @pl.when(high == 1)
        def _():
            pass_two[c].wait_send()

        @pl.when(odd == 0)
        def _():
            own_one[c].wait_send()

        @pl.when(odd == 1)
        def _():
            pass_four[c].wait_send()


def shards(n, features, img_weight, text_embed, log_scale, logit_bias):
    tok, depth = features.shape
    part = img_weight.shape[1]
    vmem = pl.BlockSpec(memory_space=pltpu.VMEM)
    smem = pl.BlockSpec(memory_space=pltpu.SMEM)

    def block(dtype, *lead):
        return pltpu.VMEM((*lead, part, tok), dtype)

    def piece(size, dtype=BF16, *lead):
        return pltpu.VMEM((*lead, size, depth), dtype)

    levels = 1
    while 8 << levels < n:
        levels += 1
    dma = pltpu.SemaphoreType.DMA
    pairs = STEPS + 1
    half, quarter = part // 2, part // 4
    eighth = (quarter // 2 + 15) // 16 * 16
    row = pltpu.VMEM((8, tok), F32)
    img_grad, txt_grad, weight_grad = pl.pallas_call(
        functools.partial(kernel, n),
        out_shape=(
            jax.ShapeDtypeStruct((part, tok), BF16),
            jax.ShapeDtypeStruct((part, tok), BF16),
            jax.ShapeDtypeStruct((part, depth), BF16),
        ),
        in_specs=[vmem, vmem, vmem, smem, smem],
        out_specs=(vmem, vmem, vmem),
        scratch_shapes=[
            block(F32), block(BF16), pltpu.VMEM((tok, part), BF16), row,
            block(BF16, pairs), pltpu.VMEM((pairs, 8, tok), F32), row,
            block(F32), block(F32), pltpu.VMEM((tok, tok), F32),
            pltpu.VMEM((pairs, tok, tok), F32),
            pltpu.VMEM((pairs, tok + TAIL, tok), BF16), pltpu.VMEM((pairs, tok + TAIL, tok), BF16),
            block(BF16, 4), block(BF16, 2), block(BF16), block(BF16), block(BF16), block(BF16),
            piece(half, F32), piece(half), piece(half), piece(quarter), piece(quarter),
            piece(eighth), piece(eighth), piece(eighth, BF16, levels), piece(eighth, BF16, levels),
            pltpu.VMEM((2, 8, tok), F32), pltpu.VMEM((2, 8, tok), F32),
            dma((4, CHUNKS)), dma((pairs, CHUNKS)), dma((pairs,)), dma((pairs,)), dma((4,)), dma((4,)),
            dma((6 + levels,)), dma((6 + levels,)), dma((2,)), dma((2,)),
        ],
        compiler_params=pltpu.CompilerParams(
            collective_id=0, has_side_effects=True, vmem_limit_bytes=48 * 1024 * 1024
        ),
    )(features, img_weight.T, text_embed.T, log_scale, logit_bias)
    return img_grad.T, txt_grad.T, weight_grad.T


def solution(mesh):
    in_specs = (P("dp", None), P(None, "rep"), P("dp", "rep"), P(), P())
    out_specs = (P("dp", "rep"), P("dp", "rep"), P(None, "rep"))
    body = functools.partial(shards, mesh.shape["dp"])
    return jax.shard_map(body, mesh=mesh, in_specs=in_specs, out_specs=out_specs, check_vma=False)
```

```python
import functools

import jax
import jax.numpy as jnp
from jax import lax
from jax.experimental import pallas as pl
from jax.experimental.pallas import tpu as pltpu
from jax.sharding import PartitionSpec as P

STEPS = 4
CHUNKS = 4
TAIL = 16
EPSILON = 1e-06
F32 = jnp.float32
BF16 = jnp.bfloat16
MESH = pl.DeviceIdType.MESH


def kernel(
    n, features_hbm, weight_hbm, text_hbm, log_scale, bias, img_out, txt_out, w_out,
    features, weight, text,
    img_hat, img_bf, img_rows, img_inv, span, squares, inverses, d_img, d_txt, dots,
    own_score, score_out, score_in, back, from_core, sum_two, sum_four, two_in, four_in,
    acc, half_out, half_in, quarter_out, quarter_in, eighth_out, eighth_in,
    last_out, last_in, rows_out, rows_in,
    s_span, r_span, s_score, r_score, s_back, r_back, s_w, r_w, s_rows, r_rows, s_local,
):
    k = lax.axis_index("dp")
    x = lax.axis_index("rep")
    tok = features.shape[0]
    part = weight.shape[0]
    odd = lax.rem(k, 2)
    high = lax.rem(k // 2, 2)

    def bit(b):
        return lax.rem(k // b, 2)

    def flip(b):
        return k + b - 2 * b * bit(b)

    def at(offset):
        return (lax.rem(k + offset + n, n), x)

    core = (flip(1), x)
    across = (k, 1 - x)
    far = []
    b = 8
    while b < n:
        far.append(b)
        b *= 2

    def copy(src, dst, s, r, device):
        return pltpu.make_async_remote_copy(
            src_ref=src, dst_ref=dst, send_sem=s, recv_sem=r,
            device_id=device, device_id_type=MESH,
        )

    fetches = [
        pltpu.make_async_copy(src, dst, s_local.at[i])
        for i, (src, dst) in enumerate(
            ((weight_hbm, weight), (features_hbm, features), (text_hbm, text))
        )
    ]
    for fetch in fetches:
        fetch.start()
    barrier = pltpu.get_barrier_semaphore()
    friends = [across, core, at(2), at(-2), at(4), at(-4)] + [(flip(b), x) for b in far]
    for friend in friends:
        pl.semaphore_signal(barrier, inc=1, device_id=friend, device_id_type=MESH)
    pl.semaphore_wait(barrier, len(friends))

    size = part // CHUNKS

    def text_copy(source, target, c, device, i):
        piece = pl.ds(c * size, size)
        src = text_hbm if source is None else span.at[source]
        return copy(
            src.at[piece], span.at[target, piece], s_span.at[i, c], r_span.at[target, c], device
        )

    def arrived(s, c):
        piece = pl.ds(c * size, size)
        copy(
            span.at[s, piece], span.at[s, piece], s_span.at[0, c], r_span.at[s, c], core
        ).wait_recv()

    slot = 3 - 2 * odd
    own_four = [text_copy(None, 4, c, at(4), 0) for c in range(CHUNKS)]
    own_two = [text_copy(None, 2, c, at(2), 1) for c in range(CHUNKS)]
    pass_two = [text_copy(4, 2, c, at(-2), 1) for c in range(CHUNKS)]
    own_one = [text_copy(None, 1, c, core, 2) for c in range(CHUNKS)]
    pass_four = [text_copy(4, 3, c, core, 2) for c in range(CHUNKS)]
    share_two = [text_copy(2, slot, c, core, 3) for c in range(CHUNKS)]

    for c in range(CHUNKS):
        own_four[c].start()

        @pl.when(high == 0)
        def _():
            own_two[c].start()

        @pl.when(odd == 0)
        def _():
            own_one[c].start()

    def along(a, b):
        return lax.dot_general(a, b, (((1,), (1,)), ((), ())), preferred_element_type=F32)

    for fetch in fetches:
        fetch.wait()
    raw = along(weight[...], features[...])
    img_hat[...] = raw
    mine = jnp.sum(raw * raw, axis=0, keepdims=True)
    rows_out[0] = jnp.broadcast_to(mine, (8, tok))
    c = copy(rows_out.at[0], rows_in.at[0], s_rows.at[0], r_rows.at[0], across)
    c.start()
    t_wide = jnp.exp(jnp.full((1, tok), log_scale[0], F32))
    c.wait()
    inverse = lax.rsqrt(mine + rows_in[0, 0:1, :] + EPSILON)
    img_inv[...] = jnp.broadcast_to(inverse, (8, tok))
    hat = img_hat[...] * inverse
    img_hat[...] = hat
    img_bf[...] = hat.astype(BF16)
    img_rows[...] = jnp.transpose(img_bf[...])

    def text_of(s):
        return text[...] if isinstance(s, int) and s == 0 else span[s]

    def score_copy(s):
        return copy(score_out.at[s], score_in.at[s], s_score.at[s], r_score.at[s], across)

    def begin(s):
        block = text_of(s)
        score = jnp.dot(img_rows[...], block, preferred_element_type=F32)
        own_score[s] = score
        score_out[s, 0:tok, :] = score.astype(BF16)
        wide = block.astype(F32)
        square = jnp.sum(wide * wide, axis=0, keepdims=True)
        squares[s] = jnp.broadcast_to(square, (8, tok))
        top = square.astype(BF16).astype(F32)
        middle = (square - top).astype(BF16).astype(F32)
        low = square - top - middle
        row = lax.broadcasted_iota(jnp.int32, (TAIL, tok), 0)
        tail = jnp.where(row == 0, top, jnp.where(row == 1, middle, low))
        score_out[s, tok : tok + TAIL, :] = tail.astype(BF16)
        score_copy(s).start()

    def finish(s, first=False):
        score_copy(s).wait()
        tail = score_in[s, tok : tok + TAIL, :].astype(F32)
        square = squares[s, 0:1, :] + (tail[0:1] + tail[1:2] + tail[2:3])
        inverse = lax.rsqrt(square + EPSILON)
        if first:
            inverses[...] = jnp.broadcast_to(inverse, (8, tok))
        score = (own_score[s] + score_in[s, 0:tok, :].astype(F32)) * inverse
        g = jax.nn.sigmoid(t_wide * score + bias[0])
        if first:
            row = lax.broadcasted_iota(jnp.int32, (tok, tok), 0)
            col = lax.broadcasted_iota(jnp.int32, (tok, tok), 1)
            g = g - jnp.where(row == col, 1.0, 0.0)
        term = along(text_of(s), (g * inverse).astype(BF16))
        if first:
            d_img[...] = term
            dots[...] = g * score
        else:
            d_img[...] += term
            dots[...] += g * score
        return g.astype(BF16)

    def returned(g):
        return jnp.dot(img_bf[...], g, preferred_element_type=F32)

    def core_copy(i):
        return copy(back.at[2 * i], from_core.at[i], s_back.at[i], r_back.at[i], core)

    def choose(for_even, for_odd):
        return for_even + odd * (for_odd - for_even)

    oddf = odd.astype(F32)
    highf = high.astype(F32)
    send_two = copy(sum_two, two_in, s_back.at[2], r_back.at[2], (flip(2), x))
    send_four = copy(sum_four, four_in, s_back.at[3], r_back.at[3], at(-4))
    second, third, fifth = choose(4, 1), choose(3, 4), choose(1, 3)

    begin(0)

    @pl.when(odd == 1)
    def _():
        for c in range(CHUNKS):
            arrived(1, c)

    @pl.when(odd == 0)
    def _():
        for c in range(CHUNKS):
            arrived(4, c)

            @pl.when(high == 1)
            def _():
                pass_two[c].start()

    begin(second)
    d_txt[...] = returned(finish(0, True))

    @pl.when(odd == 1)
    def _():
        for c in range(CHUNKS):
            arrived(4, c)
            pass_four[c].start()

            @pl.when(high == 1)
            def _():
                pass_two[c].start()

    @pl.when(odd == 0)
    def _():
        for c in range(CHUNKS):
            arrived(3, c)

    begin(third)
    back[second - 1] = returned(finish(second)).astype(BF16)

    @pl.when(odd == 1)
    def _():
        core_copy(0).start()

    for c in range(CHUNKS):
        arrived(2, c)
        share_two[c].start()
    begin(2)
    back[third - 1] = returned(finish(third)).astype(BF16)

    @pl.when(odd == 0)
    def _():
        core_copy(1).start()

    for c in range(CHUNKS):
        arrived(fifth, c)
    begin(fifth)
    back[1] = returned(finish(2)).astype(BF16)

    @pl.when(odd == 0)
    def _():
        sum_four[...] = back[3]

    @pl.when(odd == 1)
    def _():
        core_copy(1).wait_recv()
        sum_four[...] = (back[3].astype(F32) + from_core[1].astype(F32)).astype(BF16)

    @pl.when(high == 0)
    def _():
        send_four.start()

    last_g = finish(fifth)

    dot = jnp.sum(jnp.transpose(dots[...]), axis=0, keepdims=True)
    grad = (d_img[...] - img_hat[...] * dot) * (t_wide * img_inv[0:1, :])
    img_out[...] = grad.astype(BF16)

    half, quarter = part // 2, part // 4
    eighth = (quarter // 2 + 15) // 16 * 16
    rest = quarter - eighth

    def rows(start, size):
        return pl.ds(pl.multiple_of(start, 16), size)

    half_out[...] = jnp.dot(
        img_out[rows((1 - odd) * half, half), :], features[...], preferred_element_type=F32
    ).astype(BF16)
    one = copy(half_out, half_in, s_w.at[0], r_w.at[0], core)
    one.start()
    back[fifth - 1] = returned(last_g).astype(BF16)

    @pl.when(odd == 0)
    def _():
        core_copy(0).start()

    @pl.when(odd == 1)
    def _():
        core_copy(1).start()

    acc[...] = jnp.dot(img_out[rows(odd * half, half), :], features[...], preferred_element_type=F32)

    core_copy(0).wait_recv()

    @pl.when(odd == 0)
    def _():
        core_copy(1).wait_recv()

    sum_two[...] = (back[1].astype(F32) + from_core[1 - odd].astype(F32)).astype(BF16)
    send_two.start()

    first_b, second_b = 2 + 2 * odd, 4 - 2 * odd
    first_bit = high * (1 - odd) + bit(4) * odd
    second_bit = high * odd + bit(4) * (1 - odd)
    first_peer = (k + first_b - 2 * first_b * first_bit, x)
    second_peer = (k + second_b - 2 * second_b * second_bit, x)

    one.wait()
    acc[...] += half_in[...].astype(F32)
    quarter_out[...] = acc[rows((1 - first_bit) * quarter, quarter), :].astype(BF16)
    two = copy(quarter_out, quarter_in, s_w.at[1], r_w.at[1], first_peer)
    two.start()

    two.wait()
    keep = first_bit * quarter
    acc[rows(keep, quarter), :] += quarter_in[...].astype(F32)
    eighth_out[...] = acc[rows(keep + (1 - second_bit) * rest, eighth), :].astype(BF16)
    three = copy(eighth_out, eighth_in, s_w.at[2], r_w.at[2], second_peer)
    three.start()
    send_two.wait()

    @pl.when(high == 1)
    def _():
        sum_four[...] = (
            back[3].astype(F32) + from_core[1].astype(F32) * oddf + two_in[...].astype(F32)
        ).astype(BF16)
        send_four.start()

    three.wait()
    total = acc[rows(keep + second_bit * rest, eighth), :] + eighth_in[...].astype(F32)
    for i, b in enumerate(far):
        last_out[i] = total.astype(BF16)
        c = copy(last_out.at[i], last_in.at[i], s_w.at[6 + i], r_w.at[6 + i], (flip(b), x))
        c.start()
        c.wait()
        total = last_out[i].astype(F32) + last_in[i].astype(F32)
    last_out[0] = total.astype(BF16)
    base = odd * half + keep

    def spread(i, start, size, device):
        piece = w_out.at[rows(start, size), :]
        return copy(piece, piece, s_w.at[i], r_w.at[i], device)

    def landed(i, start, size):
        piece = w_out.at[rows(start, size), :]
        copy(piece, piece, s_w.at[i], r_w.at[i], core).wait_recv()

    @pl.when(second_bit == 0)
    def _():
        w_out[rows(base, eighth), :] = last_out[0]
        spread(3, base, eighth, second_peer).start()

    @pl.when(second_bit == 1)
    def _():
        w_out[rows(base + eighth, rest), :] = last_out[0, eighth - rest :, :]
        spread(3, base + eighth, rest, second_peer).start()

    @pl.when(second_bit == 0)
    def _():
        spread(3, base, eighth, second_peer).wait_send()
        landed(3, base + eighth, rest)

    @pl.when(second_bit == 1)
    def _():
        spread(3, base + eighth, rest, second_peer).wait_send()
        landed(3, base, eighth)

    c4 = spread(4, base, quarter, first_peer)
    c4.start()

    landed(4, odd * half + (1 - first_bit) * quarter, quarter)
    c5 = spread(5, odd * half, half, core)
    c5.start()

    send_four.wait()
    even = 1.0 - oddf
    grad = (
        d_txt[...] + four_in[...].astype(F32) + from_core[0].astype(F32) * even
        + two_in[...].astype(F32) * (1.0 - highf)
    )
    d_txt[...] = grad
    hat = text[...].astype(F32) * inverses[0:1, :]
    dot = jnp.sum(hat * grad, axis=0, keepdims=True)
    rows_out[1] = jnp.broadcast_to(dot, (8, tok))
    cd = copy(rows_out.at[1], rows_in.at[1], s_rows.at[1], r_rows.at[1], across)
    cd.start()
    cd.wait()
    dot = dot + rows_in[1, 0:1, :]
    inverse = inverses[0:1, :]
    hat = text[...].astype(F32) * inverse
    txt_out[...] = ((d_txt[...] - hat * dot) * (t_wide * inverse)).astype(BF16)

    landed(5, (1 - odd) * half, half)
    c4.wait_send()
    c5.wait_send()
    core_copy(0).wait_send()
    core_copy(1).wait_send()
    for c in range(CHUNKS):
        own_four[c].wait_send()
        share_two[c].wait_send()

        @pl.when(high == 0)
        def _():
            own_two[c].wait_send()

        @pl.when(high == 1)
        def _():
            pass_two[c].wait_send()

        @pl.when(odd == 0)
        def _():
            own_one[c].wait_send()

        @pl.when(odd == 1)
        def _():
            pass_four[c].wait_send()


def shards(n, features, img_weight, text_embed, log_scale, logit_bias):
    tok, depth = features.shape
    part = img_weight.shape[1]
    vmem = pl.BlockSpec(memory_space=pltpu.VMEM)
    anywhere = pl.BlockSpec(memory_space=pl.ANY)
    smem = pl.BlockSpec(memory_space=pltpu.SMEM)

    def block(dtype, *lead):
        return pltpu.VMEM((*lead, part, tok), dtype)

    def piece(size, dtype=BF16, *lead):
        return pltpu.VMEM((*lead, size, depth), dtype)

    levels = 1
    while 8 << levels < n:
        levels += 1
    dma = pltpu.SemaphoreType.DMA
    pairs = STEPS + 1
    half, quarter = part // 2, part // 4
    eighth = (quarter // 2 + 15) // 16 * 16
    row = pltpu.VMEM((8, tok), F32)
    img_grad, txt_grad, weight_grad = pl.pallas_call(
        functools.partial(kernel, n),
        out_shape=(
            jax.ShapeDtypeStruct((part, tok), BF16),
            jax.ShapeDtypeStruct((part, tok), BF16),
            jax.ShapeDtypeStruct((part, depth), BF16),
        ),
        in_specs=[anywhere, anywhere, anywhere, smem, smem],
        out_specs=(vmem, vmem, vmem),
        scratch_shapes=[
            pltpu.VMEM((tok, depth), BF16), piece(part), block(BF16),
            block(F32), block(BF16), pltpu.VMEM((tok, part), BF16), row,
            block(BF16, pairs), pltpu.VMEM((pairs, 8, tok), F32), row,
            block(F32), block(F32), pltpu.VMEM((tok, tok), F32),
            pltpu.VMEM((pairs, tok, tok), F32),
            pltpu.VMEM((pairs, tok + TAIL, tok), BF16), pltpu.VMEM((pairs, tok + TAIL, tok), BF16),
            block(BF16, 4), block(BF16, 2), block(BF16), block(BF16), block(BF16), block(BF16),
            piece(half, F32), piece(half), piece(half), piece(quarter), piece(quarter),
            piece(eighth), piece(eighth), piece(eighth, BF16, levels), piece(eighth, BF16, levels),
            pltpu.VMEM((2, 8, tok), F32), pltpu.VMEM((2, 8, tok), F32),
            dma((4, CHUNKS)), dma((pairs, CHUNKS)), dma((pairs,)), dma((pairs,)), dma((4,)), dma((4,)),
            dma((6 + levels,)), dma((6 + levels,)), dma((2,)), dma((2,)), dma((3,)),
        ],
        compiler_params=pltpu.CompilerParams(
            collective_id=0, has_side_effects=True, vmem_limit_bytes=62 * 1024 * 1024
        ),
    )(features, img_weight.T, text_embed.T, log_scale, logit_bias)
    return img_grad.T, txt_grad.T, weight_grad.T


def solution(mesh):
    in_specs = (P("dp", None), P(None, "rep"), P("dp", "rep"), P(), P())
    out_specs = (P("dp", "rep"), P("dp", "rep"), P(None, "rep"))
    body = functools.partial(shards, mesh.shape["dp"])
    return jax.shard_map(body, mesh=mesh, in_specs=in_specs, out_specs=out_specs, check_vma=False)
```

```python
import functools

import jax
import jax.numpy as jnp
from jax import lax
from jax.experimental import pallas as pl
from jax.experimental.pallas import tpu as pltpu
from jax.sharding import PartitionSpec as P

STEPS = 4
CHUNKS = 4
TAIL = 16
EPSILON = 1e-06
F32 = jnp.float32
BF16 = jnp.bfloat16
MESH = pl.DeviceIdType.MESH


def kernel(
    n, features_hbm, weight_hbm, text_hbm, log_scale, bias, img_out, txt_out, w_out,
    features, weight, text,
    img_hat, img_bf, img_rows, img_inv, span, squares, inverses, d_img, d_txt, dots,
    own_score, score_out, score_in, back, from_core, sum_two, sum_four, two_in, four_in,
    acc, core_grad, core_features, quarter_out, quarter_in, eighth_out, eighth_in,
    last_out, last_in, rows_out, rows_in,
    s_span, r_span, s_score, r_score, s_back, r_back, s_w, r_w, s_rows, r_rows, s_local,
):
    k = lax.axis_index("dp")
    x = lax.axis_index("rep")
    tok = features.shape[0]
    part = weight.shape[0]
    odd = lax.rem(k, 2)
    high = lax.rem(k // 2, 2)

    def bit(b):
        return lax.rem(k // b, 2)

    def flip(b):
        return k + b - 2 * b * bit(b)

    def at(offset):
        return (lax.rem(k + offset + n, n), x)

    core = (flip(1), x)
    across = (k, 1 - x)
    far = []
    b = 8
    while b < n:
        far.append(b)
        b *= 2

    def copy(src, dst, s, r, device):
        return pltpu.make_async_remote_copy(
            src_ref=src, dst_ref=dst, send_sem=s, recv_sem=r,
            device_id=device, device_id_type=MESH,
        )

    fetches = [
        pltpu.make_async_copy(src, dst, s_local.at[i])
        for i, (src, dst) in enumerate(
            ((weight_hbm, weight), (features_hbm, features), (text_hbm, text))
        )
    ]
    for fetch in fetches:
        fetch.start()
    barrier = pltpu.get_barrier_semaphore()
    friends = [across, core, at(2), at(-2), at(4), at(-4)] + [(flip(b), x) for b in far]
    for friend in friends:
        pl.semaphore_signal(barrier, inc=1, device_id=friend, device_id_type=MESH)
    pl.semaphore_wait(barrier, len(friends))

    size = part // CHUNKS

    def text_copy(source, target, c, device, i):
        piece = pl.ds(c * size, size)
        src = text_hbm if source is None else span.at[source]
        return copy(
            src.at[piece], span.at[target, piece], s_span.at[i, c], r_span.at[target, c], device
        )

    def arrived(s, c):
        piece = pl.ds(c * size, size)
        copy(
            span.at[s, piece], span.at[s, piece], s_span.at[0, c], r_span.at[s, c], core
        ).wait_recv()

    slot = 3 - 2 * odd
    own_four = [text_copy(None, 4, c, at(4), 0) for c in range(CHUNKS)]
    own_two = [text_copy(None, 2, c, at(2), 1) for c in range(CHUNKS)]
    pass_two = [text_copy(4, 2, c, at(-2), 1) for c in range(CHUNKS)]
    own_one = [text_copy(None, 1, c, core, 2) for c in range(CHUNKS)]
    pass_four = [text_copy(4, 3, c, core, 2) for c in range(CHUNKS)]
    share_two = [text_copy(2, slot, c, core, 3) for c in range(CHUNKS)]

    for c in range(CHUNKS):
        own_four[c].start()

        @pl.when(high == 0)
        def _():
            own_two[c].start()

        @pl.when(odd == 0)
        def _():
            own_one[c].start()

    core_features_copy = copy(features_hbm, core_features, s_rows.at[2], r_rows.at[2], core)
    core_features_copy.start()

    def along(a, b):
        return lax.dot_general(a, b, (((1,), (1,)), ((), ())), preferred_element_type=F32)

    for fetch in fetches:
        fetch.wait()
    raw = along(weight[...], features[...])
    img_hat[...] = raw
    mine = jnp.sum(raw * raw, axis=0, keepdims=True)
    rows_out[0] = jnp.broadcast_to(mine, (8, tok))
    c = copy(rows_out.at[0], rows_in.at[0], s_rows.at[0], r_rows.at[0], across)
    c.start()
    t_wide = jnp.exp(jnp.full((1, tok), log_scale[0], F32))
    c.wait()
    inverse = lax.rsqrt(mine + rows_in[0, 0:1, :] + EPSILON)
    img_inv[...] = jnp.broadcast_to(inverse, (8, tok))
    hat = img_hat[...] * inverse
    img_hat[...] = hat
    img_bf[...] = hat.astype(BF16)
    img_rows[...] = jnp.transpose(img_bf[...])

    def text_of(s):
        return text[...] if isinstance(s, int) and s == 0 else span[s]

    def score_copy(s):
        return copy(score_out.at[s], score_in.at[s], s_score.at[s], r_score.at[s], across)

    def begin(s):
        block = text_of(s)
        score = jnp.dot(img_rows[...], block, preferred_element_type=F32)
        own_score[s] = score
        score_out[s, 0:tok, :] = score.astype(BF16)
        wide = block.astype(F32)
        square = jnp.sum(wide * wide, axis=0, keepdims=True)
        squares[s] = jnp.broadcast_to(square, (8, tok))
        top = square.astype(BF16).astype(F32)
        middle = (square - top).astype(BF16).astype(F32)
        low = square - top - middle
        row = lax.broadcasted_iota(jnp.int32, (TAIL, tok), 0)
        tail = jnp.where(row == 0, top, jnp.where(row == 1, middle, low))
        score_out[s, tok : tok + TAIL, :] = tail.astype(BF16)
        score_copy(s).start()

    def finish(s, first=False):
        score_copy(s).wait()
        tail = score_in[s, tok : tok + TAIL, :].astype(F32)
        square = squares[s, 0:1, :] + (tail[0:1] + tail[1:2] + tail[2:3])
        inverse = lax.rsqrt(square + EPSILON)
        if first:
            inverses[...] = jnp.broadcast_to(inverse, (8, tok))
        score = (own_score[s] + score_in[s, 0:tok, :].astype(F32)) * inverse
        g = jax.nn.sigmoid(t_wide * score + bias[0])
        if first:
            row = lax.broadcasted_iota(jnp.int32, (tok, tok), 0)
            col = lax.broadcasted_iota(jnp.int32, (tok, tok), 1)
            g = g - jnp.where(row == col, 1.0, 0.0)
        term = along(text_of(s), (g * inverse).astype(BF16))
        if first:
            d_img[...] = term
            dots[...] = g * score
        else:
            d_img[...] += term
            dots[...] += g * score
        return g.astype(BF16)

    def returned(g):
        return jnp.dot(img_bf[...], g, preferred_element_type=F32)

    def core_copy(i):
        return copy(back.at[2 * i], from_core.at[i], s_back.at[i], r_back.at[i], core)

    def choose(for_even, for_odd):
        return for_even + odd * (for_odd - for_even)

    oddf = odd.astype(F32)
    highf = high.astype(F32)
    send_two = copy(sum_two, two_in, s_back.at[2], r_back.at[2], (flip(2), x))
    send_four = copy(sum_four, four_in, s_back.at[3], r_back.at[3], at(-4))
    second, third, fifth = choose(4, 1), choose(3, 4), choose(1, 3)

    begin(0)

    @pl.when(odd == 1)
    def _():
        for c in range(CHUNKS):
            arrived(1, c)

    @pl.when(odd == 0)
    def _():
        for c in range(CHUNKS):
            arrived(4, c)

            @pl.when(high == 1)
            def _():
                pass_two[c].start()

    begin(second)
    d_txt[...] = returned(finish(0, True))

    @pl.when(odd == 1)
    def _():
        for c in range(CHUNKS):
            arrived(4, c)
            pass_four[c].start()

            @pl.when(high == 1)
            def _():
                pass_two[c].start()

    @pl.when(odd == 0)
    def _():
        for c in range(CHUNKS):
            arrived(3, c)

    begin(third)
    back[second - 1] = returned(finish(second)).astype(BF16)

    @pl.when(odd == 1)
    def _():
        core_copy(0).start()

    for c in range(CHUNKS):
        arrived(2, c)
        share_two[c].start()
    begin(2)
    back[third - 1] = returned(finish(third)).astype(BF16)

    @pl.when(odd == 0)
    def _():
        core_copy(1).start()

    for c in range(CHUNKS):
        arrived(fifth, c)
    begin(fifth)
    back[1] = returned(finish(2)).astype(BF16)

    @pl.when(odd == 0)
    def _():
        sum_four[...] = back[3]

    @pl.when(odd == 1)
    def _():
        core_copy(1).wait_recv()
        sum_four[...] = (back[3].astype(F32) + from_core[1].astype(F32)).astype(BF16)

    @pl.when(high == 0)
    def _():
        send_four.start()

    last_g = finish(fifth)

    dot = jnp.sum(jnp.transpose(dots[...]), axis=0, keepdims=True)
    grad = (d_img[...] - img_hat[...] * dot) * (t_wide * img_inv[0:1, :])
    img_out[...] = grad.astype(BF16)

    half, quarter = part // 2, part // 4
    eighth = (quarter // 2 + 15) // 16 * 16
    rest = quarter - eighth
    depth = features.shape[1]
    cut = (depth // 2 + 127) // 128 * 128
    streams = (pl.ds(0, cut), pl.ds(cut, depth - cut))
    both = range(2)

    def rows(start, size):
        return pl.ds(pl.multiple_of(start, 16), size)

    swap = copy(
        img_out.at[rows((1 - odd) * half, half), :], core_grad, s_w.at[0], r_w.at[0], core
    )
    swap.start()
    back[fifth - 1] = returned(last_g).astype(BF16)

    @pl.when(odd == 0)
    def _():
        core_copy(0).start()

    @pl.when(odd == 1)
    def _():
        core_copy(1).start()

    first_b, second_b = 2 + 2 * odd, 4 - 2 * odd
    first_bit = high * (1 - odd) + bit(4) * odd
    second_bit = high * odd + bit(4) * (1 - odd)
    first_peer = (k + first_b - 2 * first_b * first_bit, x)
    second_peer = (k + second_b - 2 * second_b * second_bit, x)
    keep = first_bit * quarter
    mine_at = keep + second_bit * rest
    base = odd * half + keep

    def stage(i, u, src, dst, device):
        lanes = streams[u]
        return copy(
            src.at[:, lanes], dst.at[:, lanes], s_w.at[1 + 2 * i + u], r_w.at[1 + 2 * i + u], device
        )

    acc[...] = jnp.dot(img_out[rows(odd * half, half), :], features[...], preferred_element_type=F32)
    swap.wait()
    core_features_copy.wait()
    two, three = [], []
    for u in both:
        lanes = streams[u]
        acc[:, lanes] += jnp.dot(
            core_grad[...], core_features[:, lanes], preferred_element_type=F32
        )
        quarter_out[:, lanes] = acc[rows((1 - first_bit) * quarter, quarter), lanes].astype(BF16)
        two.append(stage(0, u, quarter_out, quarter_in, first_peer))
        two[u].start()

    core_copy(0).wait_recv()

    @pl.when(odd == 0)
    def _():
        core_copy(1).wait_recv()

    sum_two[...] = (back[1].astype(F32) + from_core[1 - odd].astype(F32)).astype(BF16)
    send_two.start()

    for u in both:
        lanes = streams[u]
        two[u].wait()
        acc[rows(keep, quarter), lanes] += quarter_in[:, lanes].astype(F32)
        eighth_out[:, lanes] = acc[
            rows(keep + (1 - second_bit) * rest, eighth), lanes
        ].astype(BF16)
        three.append(stage(1, u, eighth_out, eighth_in, second_peer))
        three[u].start()

    def exchange(i, u):
        return stage(5 + i, u, last_out.at[i], last_in.at[i], (flip(far[i]), x))

    for u in both:
        lanes = streams[u]
        three[u].wait()
        total = acc[rows(mine_at, eighth), lanes] + eighth_in[:, lanes].astype(F32)
        last_out[0, :, lanes] = total.astype(BF16)
        if far:
            exchange(0, u).start()

    send_two.wait()

    @pl.when(high == 1)
    def _():
        sum_four[...] = (
            back[3].astype(F32) + from_core[1].astype(F32) * oddf + two_in[...].astype(F32)
        ).astype(BF16)
        send_four.start()

    def spread(i, u, start, size, device):
        piece = w_out.at[rows(start, size), streams[u]]
        return copy(piece, piece, s_w.at[1 + 2 * i + u], r_w.at[1 + 2 * i + u], device)

    for i in range(len(far)):
        for u in both:
            lanes = streams[u]
            exchange(i, u).wait()
            total = last_out[i, :, lanes].astype(F32) + last_in[i, :, lanes].astype(F32)
            last_out[i + 1, :, lanes] = total.astype(BF16)
            if i + 1 < len(far):
                exchange(i + 1, u).start()

    for u in both:
        lanes = streams[u]

        @pl.when(second_bit == 0)
        def _():
            w_out[rows(base, eighth), lanes] = last_out[len(far), :, lanes]
            spread(2, u, base, eighth, second_peer).start()

        @pl.when(second_bit == 1)
        def _():
            w_out[rows(base + eighth, rest), lanes] = last_out[len(far), eighth - rest :, lanes]
            spread(2, u, base + eighth, rest, second_peer).start()

    for u in both:

        @pl.when(second_bit == 0)
        def _():
            spread(2, u, base, eighth, second_peer).wait_send()
            spread(2, u, base + eighth, rest, second_peer).wait_recv()

        @pl.when(second_bit == 1)
        def _():
            spread(2, u, base + eighth, rest, second_peer).wait_send()
            spread(2, u, base, eighth, second_peer).wait_recv()

        spread(3, u, base, quarter, first_peer).start()

    for u in both:
        spread(3, u, odd * half + (1 - first_bit) * quarter, quarter, first_peer).wait_recv()
        spread(4, u, odd * half, half, core).start()

    send_four.wait()
    even = 1.0 - oddf
    grad = (
        d_txt[...] + four_in[...].astype(F32) + from_core[0].astype(F32) * even
        + two_in[...].astype(F32) * (1.0 - highf)
    )
    d_txt[...] = grad
    hat = text[...].astype(F32) * inverses[0:1, :]
    dot = jnp.sum(hat * grad, axis=0, keepdims=True)
    rows_out[1] = jnp.broadcast_to(dot, (8, tok))
    cd = copy(rows_out.at[1], rows_in.at[1], s_rows.at[1], r_rows.at[1], across)
    cd.start()
    cd.wait()
    dot = dot + rows_in[1, 0:1, :]
    inverse = inverses[0:1, :]
    hat = text[...].astype(F32) * inverse
    txt_out[...] = ((d_txt[...] - hat * dot) * (t_wide * inverse)).astype(BF16)

    for u in both:
        spread(4, u, (1 - odd) * half, half, core).wait_recv()
        spread(3, u, base, quarter, first_peer).wait_send()
        spread(4, u, odd * half, half, core).wait_send()
    core_copy(0).wait_send()
    core_copy(1).wait_send()
    for c in range(CHUNKS):
        own_four[c].wait_send()
        share_two[c].wait_send()

        @pl.when(high == 0)
        def _():
            own_two[c].wait_send()

        @pl.when(high == 1)
        def _():
            pass_two[c].wait_send()

        @pl.when(odd == 0)
        def _():
            own_one[c].wait_send()

        @pl.when(odd == 1)
        def _():
            pass_four[c].wait_send()


def shards(n, features, img_weight, text_embed, log_scale, logit_bias):
    tok, depth = features.shape
    part = img_weight.shape[1]
    vmem = pl.BlockSpec(memory_space=pltpu.VMEM)
    anywhere = pl.BlockSpec(memory_space=pltpu.HBM)
    smem = pl.BlockSpec(memory_space=pltpu.SMEM)

    def block(dtype, *lead):
        return pltpu.VMEM((*lead, part, tok), dtype)

    def piece(size, dtype=BF16, *lead):
        return pltpu.VMEM((*lead, size, depth), dtype)

    levels = 1
    while 8 << levels < n:
        levels += 1
    dma = pltpu.SemaphoreType.DMA
    pairs = STEPS + 1
    half, quarter = part // 2, part // 4
    eighth = (quarter // 2 + 15) // 16 * 16
    row = pltpu.VMEM((8, tok), F32)
    img_grad, txt_grad, weight_grad = pl.pallas_call(
        functools.partial(kernel, n),
        out_shape=(
            jax.ShapeDtypeStruct((part, tok), BF16),
            jax.ShapeDtypeStruct((part, tok), BF16),
            jax.ShapeDtypeStruct((part, depth), BF16),
        ),
        in_specs=[anywhere, anywhere, anywhere, smem, smem],
        out_specs=(vmem, vmem, vmem),
        scratch_shapes=[
            pltpu.VMEM((tok, depth), BF16), piece(part), block(BF16),
            block(F32), block(BF16), pltpu.VMEM((tok, part), BF16), row,
            block(BF16, pairs), pltpu.VMEM((pairs, 8, tok), F32), row,
            block(F32), block(F32), pltpu.VMEM((tok, tok), F32),
            pltpu.VMEM((pairs, tok, tok), F32),
            pltpu.VMEM((pairs, tok + TAIL, tok), BF16), pltpu.VMEM((pairs, tok + TAIL, tok), BF16),
            block(BF16, 4), block(BF16, 2), block(BF16), block(BF16), block(BF16), block(BF16),
            piece(half, F32), pltpu.VMEM((half, tok), BF16), piece(tok), piece(quarter), piece(quarter),
            piece(eighth), piece(eighth), piece(eighth, BF16, levels + 1), piece(eighth, BF16, levels),
            pltpu.VMEM((2, 8, tok), F32), pltpu.VMEM((2, 8, tok), F32),
            dma((4, CHUNKS)), dma((pairs, CHUNKS)), dma((pairs,)), dma((pairs,)), dma((4,)), dma((4,)),
            dma((11 + 2 * levels,)), dma((11 + 2 * levels,)), dma((3,)), dma((3,)), dma((3,)),
        ],
        compiler_params=pltpu.CompilerParams(
            collective_id=0, has_side_effects=True, vmem_limit_bytes=48 * 1024 * 1024
        ),
    )(features, img_weight.T, text_embed.T, log_scale, logit_bias)
    return img_grad.T, txt_grad.T, weight_grad.T


def solution(mesh):
    in_specs = (P("dp", None), P(None, "rep"), P("dp", "rep"), P(), P())
    out_specs = (P("dp", "rep"), P("dp", "rep"), P(None, "rep"))
    body = functools.partial(shards, mesh.shape["dp"])
    return jax.shard_map(body, mesh=mesh, in_specs=in_specs, out_specs=out_specs, check_vma=False)
```

```python
import functools

import jax
import jax.numpy as jnp
from jax import lax
from jax.experimental import pallas as pl
from jax.experimental.pallas import tpu as pltpu
from jax.sharding import PartitionSpec as P

STEPS = 4
CHUNKS = 4
TAIL = 16
EPSILON = 1e-06
F32 = jnp.float32
BF16 = jnp.bfloat16
MESH = pl.DeviceIdType.MESH


def kernel(
    n, features_hbm, weight_hbm, text_hbm, log_scale, bias, img_out, txt_out, w_out,
    features, weight, text,
    img_hat, img_bf, img_rows, img_inv, span, squares, inverses, d_img, d_txt, dots,
    own_score, score_out, score_in, back, from_core, sum_two, sum_four, two_in, four_in,
    acc, core_grad, core_features, quarter_out, quarter_in, eighth_out, eighth_in,
    last_out, last_in, rows_out, rows_in,
    s_span, r_span, s_score, r_score, s_back, r_back, s_w, r_w, s_rows, r_rows, s_local,
):
    k = lax.axis_index("dp")
    x = lax.axis_index("rep")
    tok = features.shape[0]
    part = weight.shape[0]
    odd = lax.rem(k, 2)
    high = lax.rem(k // 2, 2)

    def bit(b):
        return lax.rem(k // b, 2)

    def flip(b):
        return k + b - 2 * b * bit(b)

    def at(offset):
        return (lax.rem(k + offset + n, n), x)

    core = (flip(1), x)
    across = (k, 1 - x)
    far = []
    b = 8
    while b < n:
        far.append(b)
        b *= 2

    def copy(src, dst, s, r, device):
        return pltpu.make_async_remote_copy(
            src_ref=src, dst_ref=dst, send_sem=s, recv_sem=r,
            device_id=device, device_id_type=MESH,
        )

    fetches = [
        pltpu.make_async_copy(src, dst, s_local.at[i])
        for i, (src, dst) in enumerate(
            ((weight_hbm, weight), (features_hbm, features), (text_hbm, text))
        )
    ]
    for fetch in fetches:
        fetch.start()
    barrier = pltpu.get_barrier_semaphore()
    friends = [across, core, at(2), at(-2), at(4), at(-4)] + [(flip(b), x) for b in far]
    for friend in friends:
        pl.semaphore_signal(barrier, inc=1, device_id=friend, device_id_type=MESH)
    pl.semaphore_wait(barrier, len(friends))

    size = part // CHUNKS

    def text_copy(source, target, c, device, i):
        piece = pl.ds(c * size, size)
        src = text_hbm if source is None else span.at[source]
        return copy(
            src.at[piece], span.at[target, piece], s_span.at[i, c], r_span.at[target, c], device
        )

    def arrived(s, c):
        piece = pl.ds(c * size, size)
        copy(
            span.at[s, piece], span.at[s, piece], s_span.at[0, c], r_span.at[s, c], core
        ).wait_recv()

    slot = 3 - 2 * odd
    own_four = [text_copy(None, 4, c, at(4), 0) for c in range(CHUNKS)]
    own_two = [text_copy(None, 2, c, at(2), 1) for c in range(CHUNKS)]
    pass_two = [text_copy(4, 2, c, at(-2), 1) for c in range(CHUNKS)]
    own_one = [text_copy(None, 1, c, core, 2) for c in range(CHUNKS)]
    pass_four = [text_copy(4, 3, c, core, 2) for c in range(CHUNKS)]
    share_two = [text_copy(2, slot, c, core, 3) for c in range(CHUNKS)]

    for c in range(CHUNKS):
        own_four[c].start()

        @pl.when(high == 0)
        def _():
            own_two[c].start()

        @pl.when(odd == 0)
        def _():
            own_one[c].start()

    core_features_copy = copy(features_hbm, core_features, s_rows.at[2], r_rows.at[2], core)
    core_features_copy.start()

    def along(a, b):
        return lax.dot_general(a, b, (((1,), (1,)), ((), ())), preferred_element_type=F32)

    for fetch in fetches:
        fetch.wait()
    raw = along(weight[...], features[...])
    img_hat[...] = raw
    mine = jnp.sum(raw * raw, axis=0, keepdims=True)
    rows_out[0] = jnp.broadcast_to(mine, (8, tok))
    c = copy(rows_out.at[0], rows_in.at[0], s_rows.at[0], r_rows.at[0], across)
    c.start()
    t_wide = jnp.exp(jnp.full((1, tok), log_scale[0], F32))
    c.wait()
    inverse = lax.rsqrt(mine + rows_in[0, 0:1, :] + EPSILON)
    img_inv[...] = jnp.broadcast_to(inverse, (8, tok))
    hat = img_hat[...] * inverse
    img_hat[...] = hat
    img_bf[...] = hat.astype(BF16)
    img_rows[...] = jnp.transpose(img_bf[...])

    def text_of(s):
        return text[...] if isinstance(s, int) and s == 0 else span[s]

    def score_copy(s):
        return copy(score_out.at[s], score_in.at[s], s_score.at[s], r_score.at[s], across)

    def begin(s):
        block = text_of(s)
        score = jnp.dot(img_rows[...], block, preferred_element_type=F32)
        own_score[s] = score
        score_out[s, 0:tok, :] = score.astype(BF16)
        wide = block.astype(F32)
        square = jnp.sum(wide * wide, axis=0, keepdims=True)
        squares[s] = jnp.broadcast_to(square, (8, tok))
        top = square.astype(BF16).astype(F32)
        middle = (square - top).astype(BF16).astype(F32)
        low = square - top - middle
        row = lax.broadcasted_iota(jnp.int32, (TAIL, tok), 0)
        tail = jnp.where(row == 0, top, jnp.where(row == 1, middle, low))
        score_out[s, tok : tok + TAIL, :] = tail.astype(BF16)
        score_copy(s).start()

    def finish(s, first=False):
        score_copy(s).wait()
        tail = score_in[s, tok : tok + TAIL, :].astype(F32)
        square = squares[s, 0:1, :] + (tail[0:1] + tail[1:2] + tail[2:3])
        inverse = lax.rsqrt(square + EPSILON)
        if first:
            inverses[...] = jnp.broadcast_to(inverse, (8, tok))
        score = (own_score[s] + score_in[s, 0:tok, :].astype(F32)) * inverse
        g = jax.nn.sigmoid(t_wide * score + bias[0])
        if first:
            row = lax.broadcasted_iota(jnp.int32, (tok, tok), 0)
            col = lax.broadcasted_iota(jnp.int32, (tok, tok), 1)
            g = g - jnp.where(row == col, 1.0, 0.0)
        term = along(text_of(s), (g * inverse).astype(BF16))
        if first:
            d_img[...] = term
            dots[...] = g * score
        else:
            d_img[...] += term
            dots[...] += g * score
        return g.astype(BF16)

    def returned(g):
        return jnp.dot(img_bf[...], g, preferred_element_type=F32)

    def core_copy(i):
        return copy(back.at[2 * i], from_core.at[i], s_back.at[i], r_back.at[i], core)

    def choose(for_even, for_odd):
        return for_even + odd * (for_odd - for_even)

    oddf = odd.astype(F32)
    highf = high.astype(F32)
    send_two = copy(sum_two, two_in, s_back.at[2], r_back.at[2], (flip(2), x))
    send_four = copy(sum_four, four_in, s_back.at[3], r_back.at[3], at(-4))
    second, third, fifth = choose(4, 1), choose(3, 4), choose(1, 3)

    begin(0)

    @pl.when(odd == 1)
    def _():
        for c in range(CHUNKS):
            arrived(1, c)

    @pl.when(odd == 0)
    def _():
        for c in range(CHUNKS):
            arrived(4, c)

            @pl.when(high == 1)
            def _():
                pass_two[c].start()

    begin(second)
    d_txt[...] = returned(finish(0, True))

    @pl.when(odd == 1)
    def _():
        for c in range(CHUNKS):
            arrived(4, c)
            pass_four[c].start()

            @pl.when(high == 1)
            def _():
                pass_two[c].start()

    @pl.when(odd == 0)
    def _():
        for c in range(CHUNKS):
            arrived(3, c)

    begin(third)
    back[second - 1] = returned(finish(second)).astype(BF16)

    @pl.when(odd == 1)
    def _():
        core_copy(0).start()

    for c in range(CHUNKS):
        arrived(2, c)
        share_two[c].start()
    begin(2)
    back[third - 1] = returned(finish(third)).astype(BF16)

    @pl.when(odd == 0)
    def _():
        core_copy(1).start()

    for c in range(CHUNKS):
        arrived(fifth, c)
    begin(fifth)
    back[1] = returned(finish(2)).astype(BF16)

    @pl.when(odd == 0)
    def _():
        sum_four[...] = back[3]

    @pl.when(odd == 1)
    def _():
        core_copy(1).wait_recv()
        sum_four[...] = (back[3].astype(F32) + from_core[1].astype(F32)).astype(BF16)

    @pl.when(high == 0)
    def _():
        send_four.start()

    last_g = finish(fifth)

    dot = jnp.sum(jnp.transpose(dots[...]), axis=0, keepdims=True)
    grad = (d_img[...] - img_hat[...] * dot) * (t_wide * img_inv[0:1, :])
    img_out[...] = grad.astype(BF16)

    half, quarter = part // 2, part // 4
    eighth = (quarter // 2 + 15) // 16 * 16
    rest = quarter - eighth
    depth = features.shape[1]
    cut = (depth // 2 + 127) // 128 * 128
    streams = (pl.ds(0, cut), pl.ds(cut, depth - cut))
    both = range(2)

    def rows(start, size):
        return pl.ds(pl.multiple_of(start, 16), size)

    swap = copy(
        img_out.at[rows((1 - odd) * half, half), :], core_grad, s_w.at[0], r_w.at[0], core
    )
    swap.start()
    back[fifth - 1] = returned(last_g).astype(BF16)

    @pl.when(odd == 0)
    def _():
        core_copy(0).start()

    @pl.when(odd == 1)
    def _():
        core_copy(1).start()

    first_b, second_b = 2 + 2 * odd, 4 - 2 * odd
    first_bit = high * (1 - odd) + bit(4) * odd
    second_bit = high * odd + bit(4) * (1 - odd)
    first_peer = (k + first_b - 2 * first_b * first_bit, x)
    second_peer = (k + second_b - 2 * second_b * second_bit, x)
    keep = first_bit * quarter
    mine_at = keep + second_bit * rest
    base = odd * half + keep

    def stage(i, u, src, dst, device):
        lanes = streams[u]
        return copy(
            src.at[:, lanes], dst.at[:, lanes], s_w.at[1 + 2 * i + u], r_w.at[1 + 2 * i + u], device
        )

    acc[...] = jnp.dot(img_out[rows(odd * half, half), :], features[...], preferred_element_type=F32)
    swap.wait()
    core_features_copy.wait()
    two, three = [], []
    for u in both:
        lanes = streams[u]
        acc[:, lanes] += jnp.dot(
            core_grad[...], core_features[:, lanes], preferred_element_type=F32
        )
        quarter_out[:, lanes] = acc[rows((1 - first_bit) * quarter, quarter), lanes].astype(BF16)
        two.append(stage(0, u, quarter_out, quarter_in, first_peer))
        two[u].start()

    for u in both:
        lanes = streams[u]
        two[u].wait()
        acc[rows(keep, quarter), lanes] += quarter_in[:, lanes].astype(F32)
        eighth_out[:, lanes] = acc[
            rows(keep + (1 - second_bit) * rest, eighth), lanes
        ].astype(BF16)
        three.append(stage(1, u, eighth_out, eighth_in, second_peer))
        three[u].start()

    def exchange(i, u):
        return stage(5 + i, u, last_out.at[i], last_in.at[i], (flip(far[i]), x))

    for u in both:
        lanes = streams[u]
        three[u].wait()
        total = acc[rows(mine_at, eighth), lanes] + eighth_in[:, lanes].astype(F32)
        last_out[0, :, lanes] = total.astype(BF16)
        if far:
            exchange(0, u).start()

    core_copy(0).wait_recv()

    @pl.when(odd == 0)
    def _():
        core_copy(1).wait_recv()

    sum_two[...] = (back[1].astype(F32) + from_core[1 - odd].astype(F32)).astype(BF16)
    send_two.start()

    def spread(i, u, start, size, device):
        piece = w_out.at[rows(start, size), streams[u]]
        return copy(piece, piece, s_w.at[1 + 2 * i + u], r_w.at[1 + 2 * i + u], device)

    for i in range(len(far)):
        for u in both:
            lanes = streams[u]
            exchange(i, u).wait()
            total = last_out[i, :, lanes].astype(F32) + last_in[i, :, lanes].astype(F32)
            last_out[i + 1, :, lanes] = total.astype(BF16)
            if i + 1 < len(far):
                exchange(i + 1, u).start()

    for u in both:
        lanes = streams[u]

        @pl.when(second_bit == 0)
        def _():
            w_out[rows(base, eighth), lanes] = last_out[len(far), :, lanes]
            spread(2, u, base, eighth, second_peer).start()

        @pl.when(second_bit == 1)
        def _():
            w_out[rows(base + eighth, rest), lanes] = last_out[len(far), eighth - rest :, lanes]
            spread(2, u, base + eighth, rest, second_peer).start()

    send_two.wait()

    @pl.when(high == 1)
    def _():
        sum_four[...] = (
            back[3].astype(F32) + from_core[1].astype(F32) * oddf + two_in[...].astype(F32)
        ).astype(BF16)
        send_four.start()

    for u in both:

        @pl.when(second_bit == 0)
        def _():
            spread(2, u, base, eighth, second_peer).wait_send()
            spread(2, u, base + eighth, rest, second_peer).wait_recv()

        @pl.when(second_bit == 1)
        def _():
            spread(2, u, base + eighth, rest, second_peer).wait_send()
            spread(2, u, base, eighth, second_peer).wait_recv()

        spread(3, u, base, quarter, first_peer).start()

    for u in both:
        spread(3, u, odd * half + (1 - first_bit) * quarter, quarter, first_peer).wait_recv()
        spread(4, u, odd * half, half, core).start()

    send_four.wait()
    even = 1.0 - oddf
    grad = (
        d_txt[...] + four_in[...].astype(F32) + from_core[0].astype(F32) * even
        + two_in[...].astype(F32) * (1.0 - highf)
    )
    d_txt[...] = grad
    hat = text[...].astype(F32) * inverses[0:1, :]
    dot = jnp.sum(hat * grad, axis=0, keepdims=True)
    rows_out[1] = jnp.broadcast_to(dot, (8, tok))
    cd = copy(rows_out.at[1], rows_in.at[1], s_rows.at[1], r_rows.at[1], across)
    cd.start()
    cd.wait()
    dot = dot + rows_in[1, 0:1, :]
    inverse = inverses[0:1, :]
    hat = text[...].astype(F32) * inverse
    txt_out[...] = ((d_txt[...] - hat * dot) * (t_wide * inverse)).astype(BF16)

    for u in both:
        spread(4, u, (1 - odd) * half, half, core).wait_recv()
        spread(3, u, base, quarter, first_peer).wait_send()
        spread(4, u, odd * half, half, core).wait_send()
    core_copy(0).wait_send()
    core_copy(1).wait_send()
    for c in range(CHUNKS):
        own_four[c].wait_send()
        share_two[c].wait_send()

        @pl.when(high == 0)
        def _():
            own_two[c].wait_send()

        @pl.when(high == 1)
        def _():
            pass_two[c].wait_send()

        @pl.when(odd == 0)
        def _():
            own_one[c].wait_send()

        @pl.when(odd == 1)
        def _():
            pass_four[c].wait_send()


def shards(n, features, img_weight, text_embed, log_scale, logit_bias):
    tok, depth = features.shape
    part = img_weight.shape[1]
    vmem = pl.BlockSpec(memory_space=pltpu.VMEM)
    anywhere = pl.BlockSpec(memory_space=pltpu.HBM)
    smem = pl.BlockSpec(memory_space=pltpu.SMEM)

    def block(dtype, *lead):
        return pltpu.VMEM((*lead, part, tok), dtype)

    def piece(size, dtype=BF16, *lead):
        return pltpu.VMEM((*lead, size, depth), dtype)

    levels = 1
    while 8 << levels < n:
        levels += 1
    dma = pltpu.SemaphoreType.DMA
    pairs = STEPS + 1
    half, quarter = part // 2, part // 4
    eighth = (quarter // 2 + 15) // 16 * 16
    row = pltpu.VMEM((8, tok), F32)
    held = [
        pltpu.with_memory_space_constraint(a, pltpu.HBM)
        for a in (features, img_weight.T, text_embed.T)
    ]
    img_grad, txt_grad, weight_grad = pl.pallas_call(
        functools.partial(kernel, n),
        out_shape=(
            jax.ShapeDtypeStruct((part, tok), BF16),
            jax.ShapeDtypeStruct((part, tok), BF16),
            jax.ShapeDtypeStruct((part, depth), BF16),
        ),
        in_specs=[anywhere, anywhere, anywhere, smem, smem],
        out_specs=(vmem, vmem, vmem),
        scratch_shapes=[
            pltpu.VMEM((tok, depth), BF16), piece(part), block(BF16),
            block(F32), block(BF16), pltpu.VMEM((tok, part), BF16), row,
            block(BF16, pairs), pltpu.VMEM((pairs, 8, tok), F32), row,
            block(F32), block(F32), pltpu.VMEM((tok, tok), F32),
            pltpu.VMEM((pairs, tok, tok), F32),
            pltpu.VMEM((pairs, tok + TAIL, tok), BF16), pltpu.VMEM((pairs, tok + TAIL, tok), BF16),
            block(BF16, 4), block(BF16, 2), block(BF16), block(BF16), block(BF16), block(BF16),
            piece(half, F32), pltpu.VMEM((half, tok), BF16), piece(tok), piece(quarter), piece(quarter),
            piece(eighth), piece(eighth), piece(eighth, BF16, levels + 1), piece(eighth, BF16, levels),
            pltpu.VMEM((2, 8, tok), F32), pltpu.VMEM((2, 8, tok), F32),
            dma((4, CHUNKS)), dma((pairs, CHUNKS)), dma((pairs,)), dma((pairs,)), dma((4,)), dma((4,)),
            dma((11 + 2 * levels,)), dma((11 + 2 * levels,)), dma((3,)), dma((3,)), dma((3,)),
        ],
        compiler_params=pltpu.CompilerParams(
            collective_id=0, has_side_effects=True, vmem_limit_bytes=48 * 1024 * 1024
        ),
    )(*held, log_scale, logit_bias)
    return img_grad.T, txt_grad.T, weight_grad.T


def solution(mesh):
    in_specs = (P("dp", None), P(None, "rep"), P("dp", "rep"), P(), P())
    out_specs = (P("dp", "rep"), P("dp", "rep"), P(None, "rep"))
    body = functools.partial(shards, mesh.shape["dp"])
    return jax.shard_map(body, mesh=mesh, in_specs=in_specs, out_specs=out_specs, check_vma=False)
```

```python
import functools

import jax
import jax.numpy as jnp
from jax import lax
from jax.experimental import pallas as pl
from jax.experimental.pallas import tpu as pltpu
from jax.sharding import PartitionSpec as P

STEPS = 4
CHUNKS = 4
TAIL = 16
EPSILON = 1e-06
F32 = jnp.float32
BF16 = jnp.bfloat16
MESH = pl.DeviceIdType.MESH


def kernel(
    n, features_hbm, weight_hbm, text_hbm, log_scale, bias, img_out, txt_out, w_out,
    features, weight, text,
    img_hat, img_bf, img_rows, img_inv, span, squares, inverses, d_img, d_txt, dots,
    own_score, score_out, score_in, back, from_core, sum_two, sum_four, two_in, four_in,
    acc, core_grad, core_features, quarter_out, quarter_in, eighth_out, eighth_in,
    last_out, last_in, rows_out, rows_in,
    s_span, r_span, s_score, r_score, s_back, r_back, s_w, r_w, s_rows, r_rows, s_local,
):
    k = lax.axis_index("dp")
    x = lax.axis_index("rep")
    tok = features.shape[0]
    part = weight.shape[0]
    odd = lax.rem(k, 2)
    high = lax.rem(k // 2, 2)

    def bit(b):
        return lax.rem(k // b, 2)

    def flip(b):
        return k + b - 2 * b * bit(b)

    def at(offset):
        return (lax.rem(k + offset + n, n), x)

    core = (flip(1), x)
    across = (k, 1 - x)
    far = []
    b = 8
    while b < n:
        far.append(b)
        b *= 2

    def copy(src, dst, s, r, device):
        return pltpu.make_async_remote_copy(
            src_ref=src, dst_ref=dst, send_sem=s, recv_sem=r,
            device_id=device, device_id_type=MESH,
        )

    fetches = [
        pltpu.make_async_copy(src, dst, s_local.at[i])
        for i, (src, dst) in enumerate(
            ((weight_hbm, weight), (features_hbm, features), (text_hbm, text))
        )
    ]
    for fetch in fetches:
        fetch.start()
    barrier = pltpu.get_barrier_semaphore()
    friends = [across, core, at(2), at(-2), at(4), at(-4)] + [(flip(b), x) for b in far]
    for friend in friends:
        pl.semaphore_signal(barrier, inc=1, device_id=friend, device_id_type=MESH)
    pl.semaphore_wait(barrier, len(friends))

    size = part // CHUNKS

    def text_copy(source, target, c, device, i):
        piece = pl.ds(c * size, size)
        src = text_hbm if source is None else span.at[source]
        return copy(
            src.at[piece], span.at[target, piece], s_span.at[i, c], r_span.at[target, c], device
        )

    def arrived(s, c):
        piece = pl.ds(c * size, size)
        copy(
            span.at[s, piece], span.at[s, piece], s_span.at[0, c], r_span.at[s, c], core
        ).wait_recv()

    slot = 3 - 2 * odd
    own_four = [text_copy(None, 4, c, at(4), 0) for c in range(CHUNKS)]
    own_two = [text_copy(None, 2, c, at(2), 1) for c in range(CHUNKS)]
    pass_two = [text_copy(4, 2, c, at(-2), 1) for c in range(CHUNKS)]
    own_one = [text_copy(None, 1, c, core, 2) for c in range(CHUNKS)]
    pass_four = [text_copy(4, 3, c, core, 2) for c in range(CHUNKS)]
    share_two = [text_copy(2, slot, c, core, 3) for c in range(CHUNKS)]

    for c in range(CHUNKS):
        own_four[c].start()

        @pl.when(high == 0)
        def _():
            own_two[c].start()

        @pl.when(odd == 0)
        def _():
            own_one[c].start()

    core_features_copy = copy(features_hbm, core_features, s_rows.at[2], r_rows.at[2], core)

    def along(a, b):
        return lax.dot_general(a, b, (((1,), (1,)), ((), ())), preferred_element_type=F32)

    for fetch in fetches:
        fetch.wait()
    raw = along(weight[...], features[...])
    img_hat[...] = raw
    mine = jnp.sum(raw * raw, axis=0, keepdims=True)
    rows_out[0] = jnp.broadcast_to(mine, (8, tok))
    c = copy(rows_out.at[0], rows_in.at[0], s_rows.at[0], r_rows.at[0], across)
    c.start()
    t_wide = jnp.exp(jnp.full((1, tok), log_scale[0], F32))
    c.wait()
    inverse = lax.rsqrt(mine + rows_in[0, 0:1, :] + EPSILON)
    img_inv[...] = jnp.broadcast_to(inverse, (8, tok))
    hat = img_hat[...] * inverse
    img_hat[...] = hat
    img_bf[...] = hat.astype(BF16)
    img_rows[...] = jnp.transpose(img_bf[...])

    def text_of(s):
        return text[...] if isinstance(s, int) and s == 0 else span[s]

    def score_copy(s):
        return copy(score_out.at[s], score_in.at[s], s_score.at[s], r_score.at[s], across)

    def begin(s):
        block = text_of(s)
        score = jnp.dot(img_rows[...], block, preferred_element_type=F32)
        own_score[s] = score
        score_out[s, 0:tok, :] = score.astype(BF16)
        wide = block.astype(F32)
        square = jnp.sum(wide * wide, axis=0, keepdims=True)
        squares[s] = jnp.broadcast_to(square, (8, tok))
        top = square.astype(BF16).astype(F32)
        middle = (square - top).astype(BF16).astype(F32)
        low = square - top - middle
        row = lax.broadcasted_iota(jnp.int32, (TAIL, tok), 0)
        tail = jnp.where(row == 0, top, jnp.where(row == 1, middle, low))
        score_out[s, tok : tok + TAIL, :] = tail.astype(BF16)
        score_copy(s).start()

    def finish(s, first=False):
        score_copy(s).wait()
        tail = score_in[s, tok : tok + TAIL, :].astype(F32)
        square = squares[s, 0:1, :] + (tail[0:1] + tail[1:2] + tail[2:3])
        inverse = lax.rsqrt(square + EPSILON)
        if first:
            inverses[...] = jnp.broadcast_to(inverse, (8, tok))
        score = (own_score[s] + score_in[s, 0:tok, :].astype(F32)) * inverse
        g = jax.nn.sigmoid(t_wide * score + bias[0])
        if first:
            row = lax.broadcasted_iota(jnp.int32, (tok, tok), 0)
            col = lax.broadcasted_iota(jnp.int32, (tok, tok), 1)
            g = g - jnp.where(row == col, 1.0, 0.0)
        term = along(text_of(s), (g * inverse).astype(BF16))
        if first:
            d_img[...] = term
            dots[...] = g * score
        else:
            d_img[...] += term
            dots[...] += g * score
        return g.astype(BF16)

    def returned(g):
        return jnp.dot(img_bf[...], g, preferred_element_type=F32)

    def core_copy(i):
        return copy(back.at[2 * i], from_core.at[i], s_back.at[i], r_back.at[i], core)

    def choose(for_even, for_odd):
        return for_even + odd * (for_odd - for_even)

    oddf = odd.astype(F32)
    highf = high.astype(F32)
    send_two = copy(sum_two, two_in, s_back.at[2], r_back.at[2], (flip(2), x))
    send_four = copy(sum_four, four_in, s_back.at[3], r_back.at[3], at(-4))
    second, third, fifth = choose(4, 1), choose(3, 4), choose(1, 3)

    begin(0)
    core_features_copy.start()

    @pl.when(odd == 1)
    def _():
        for c in range(CHUNKS):
            arrived(1, c)

    @pl.when(odd == 0)
    def _():
        for c in range(CHUNKS):
            arrived(4, c)

            @pl.when(high == 1)
            def _():
                pass_two[c].start()

    begin(second)

    @pl.when(odd == 1)
    def _():
        for c in range(CHUNKS):
            arrived(4, c)
            pass_four[c].start()

            @pl.when(high == 1)
            def _():
                pass_two[c].start()

    d_txt[...] = returned(finish(0, True))

    @pl.when(odd == 0)
    def _():
        for c in range(CHUNKS):
            arrived(3, c)

    begin(third)
    back[second - 1] = returned(finish(second)).astype(BF16)

    @pl.when(odd == 1)
    def _():
        core_copy(0).start()

    for c in range(CHUNKS):
        arrived(2, c)
        share_two[c].start()
    begin(2)
    back[third - 1] = returned(finish(third)).astype(BF16)

    @pl.when(odd == 0)
    def _():
        core_copy(1).start()

    for c in range(CHUNKS):
        arrived(fifth, c)
    begin(fifth)
    back[1] = returned(finish(2)).astype(BF16)

    @pl.when(odd == 0)
    def _():
        sum_four[...] = back[3]

    @pl.when(odd == 1)
    def _():
        core_copy(1).wait_recv()
        sum_four[...] = (back[3].astype(F32) + from_core[1].astype(F32)).astype(BF16)

    @pl.when(high == 0)
    def _():
        send_four.start()

    last_g = finish(fifth)

    dot = jnp.sum(jnp.transpose(dots[...]), axis=0, keepdims=True)
    grad = (d_img[...] - img_hat[...] * dot) * (t_wide * img_inv[0:1, :])
    img_out[...] = grad.astype(BF16)

    half, quarter = part // 2, part // 4
    eighth = (quarter // 2 + 15) // 16 * 16
    rest = quarter - eighth
    depth = features.shape[1]
    cut = (depth // 2 + 127) // 128 * 128
    streams = (pl.ds(0, cut), pl.ds(cut, depth - cut))
    both = range(2)

    def rows(start, size):
        return pl.ds(pl.multiple_of(start, 16), size)

    swap = copy(
        img_out.at[rows((1 - odd) * half, half), :], core_grad, s_w.at[0], r_w.at[0], core
    )
    swap.start()
    back[fifth - 1] = returned(last_g).astype(BF16)

    @pl.when(odd == 0)
    def _():
        core_copy(0).start()

    @pl.when(odd == 1)
    def _():
        core_copy(1).start()

    first_b, second_b = 2 + 2 * odd, 4 - 2 * odd
    first_bit = high * (1 - odd) + bit(4) * odd
    second_bit = high * odd + bit(4) * (1 - odd)
    first_peer = (k + first_b - 2 * first_b * first_bit, x)
    second_peer = (k + second_b - 2 * second_b * second_bit, x)
    keep = first_bit * quarter
    mine_at = keep + second_bit * rest
    base = odd * half + keep

    def stage(i, u, src, dst, device):
        lanes = streams[u]
        return copy(
            src.at[:, lanes], dst.at[:, lanes], s_w.at[1 + 2 * i + u], r_w.at[1 + 2 * i + u], device
        )

    acc[...] = jnp.dot(img_out[rows(odd * half, half), :], features[...], preferred_element_type=F32)
    swap.wait()
    core_features_copy.wait()
    two, three = [], []
    for u in both:
        lanes = streams[u]
        acc[:, lanes] += jnp.dot(
            core_grad[...], core_features[:, lanes], preferred_element_type=F32
        )
        quarter_out[:, lanes] = acc[rows((1 - first_bit) * quarter, quarter), lanes].astype(BF16)
        two.append(stage(0, u, quarter_out, quarter_in, first_peer))
        two[u].start()

    for u in both:
        lanes = streams[u]
        two[u].wait()
        acc[rows(keep, quarter), lanes] += quarter_in[:, lanes].astype(F32)
        eighth_out[:, lanes] = acc[
            rows(keep + (1 - second_bit) * rest, eighth), lanes
        ].astype(BF16)
        three.append(stage(1, u, eighth_out, eighth_in, second_peer))
        three[u].start()

    def exchange(i, u):
        return stage(5 + i, u, last_out.at[i], last_in.at[i], (flip(far[i]), x))

    for u in both:
        lanes = streams[u]
        three[u].wait()
        total = acc[rows(mine_at, eighth), lanes] + eighth_in[:, lanes].astype(F32)
        last_out[0, :, lanes] = total.astype(BF16)
        if far:
            exchange(0, u).start()

    core_copy(0).wait_recv()

    @pl.when(odd == 0)
    def _():
        core_copy(1).wait_recv()

    sum_two[...] = (back[1].astype(F32) + from_core[1 - odd].astype(F32)).astype(BF16)
    send_two.start()

    def spread(i, u, start, size, device):
        piece = w_out.at[rows(start, size), streams[u]]
        return copy(piece, piece, s_w.at[1 + 2 * i + u], r_w.at[1 + 2 * i + u], device)

    for i in range(len(far)):
        for u in both:
            lanes = streams[u]
            exchange(i, u).wait()
            total = last_out[i, :, lanes].astype(F32) + last_in[i, :, lanes].astype(F32)
            last_out[i + 1, :, lanes] = total.astype(BF16)
            if i + 1 < len(far):
                exchange(i + 1, u).start()

    for u in both:
        lanes = streams[u]

        @pl.when(second_bit == 0)
        def _():
            w_out[rows(base, eighth), lanes] = last_out[len(far), :, lanes]
            spread(2, u, base, eighth, second_peer).start()

        @pl.when(second_bit == 1)
        def _():
            w_out[rows(base + eighth, rest), lanes] = last_out[len(far), eighth - rest :, lanes]
            spread(2, u, base + eighth, rest, second_peer).start()

    send_two.wait()

    @pl.when(high == 1)
    def _():
        sum_four[...] = (
            back[3].astype(F32) + from_core[1].astype(F32) * oddf + two_in[...].astype(F32)
        ).astype(BF16)
        send_four.start()

    for u in both:

        @pl.when(second_bit == 0)
        def _():
            spread(2, u, base, eighth, second_peer).wait_send()
            spread(2, u, base + eighth, rest, second_peer).wait_recv()

        @pl.when(second_bit == 1)
        def _():
            spread(2, u, base + eighth, rest, second_peer).wait_send()
            spread(2, u, base, eighth, second_peer).wait_recv()

        spread(3, u, base, quarter, first_peer).start()

    for u in both:
        spread(3, u, odd * half + (1 - first_bit) * quarter, quarter, first_peer).wait_recv()
        spread(4, u, odd * half, half, core).start()

    send_four.wait()
    even = 1.0 - oddf
    grad = (
        d_txt[...] + four_in[...].astype(F32) + from_core[0].astype(F32) * even
        + two_in[...].astype(F32) * (1.0 - highf)
    )
    d_txt[...] = grad
    hat = text[...].astype(F32) * inverses[0:1, :]
    dot = jnp.sum(hat * grad, axis=0, keepdims=True)
    rows_out[1] = jnp.broadcast_to(dot, (8, tok))
    cd = copy(rows_out.at[1], rows_in.at[1], s_rows.at[1], r_rows.at[1], across)
    cd.start()
    cd.wait()
    dot = dot + rows_in[1, 0:1, :]
    inverse = inverses[0:1, :]
    hat = text[...].astype(F32) * inverse
    txt_out[...] = ((d_txt[...] - hat * dot) * (t_wide * inverse)).astype(BF16)

    for u in both:
        spread(4, u, (1 - odd) * half, half, core).wait_recv()
        spread(3, u, base, quarter, first_peer).wait_send()
        spread(4, u, odd * half, half, core).wait_send()
    core_copy(0).wait_send()
    core_copy(1).wait_send()
    for c in range(CHUNKS):
        own_four[c].wait_send()
        share_two[c].wait_send()

        @pl.when(high == 0)
        def _():
            own_two[c].wait_send()

        @pl.when(high == 1)
        def _():
            pass_two[c].wait_send()

        @pl.when(odd == 0)
        def _():
            own_one[c].wait_send()

        @pl.when(odd == 1)
        def _():
            pass_four[c].wait_send()


def shards(n, features, img_weight, text_embed, log_scale, logit_bias):
    tok, depth = features.shape
    part = img_weight.shape[1]
    vmem = pl.BlockSpec(memory_space=pltpu.VMEM)
    anywhere = pl.BlockSpec(memory_space=pltpu.HBM)
    smem = pl.BlockSpec(memory_space=pltpu.SMEM)

    def block(dtype, *lead):
        return pltpu.VMEM((*lead, part, tok), dtype)

    def piece(size, dtype=BF16, *lead):
        return pltpu.VMEM((*lead, size, depth), dtype)

    levels = 1
    while 8 << levels < n:
        levels += 1
    dma = pltpu.SemaphoreType.DMA
    pairs = STEPS + 1
    half, quarter = part // 2, part // 4
    eighth = (quarter // 2 + 15) // 16 * 16
    row = pltpu.VMEM((8, tok), F32)
    held = [
        pltpu.with_memory_space_constraint(a, pltpu.HBM)
        for a in (features, img_weight.T, text_embed.T)
    ]
    img_grad, txt_grad, weight_grad = pl.pallas_call(
        functools.partial(kernel, n),
        out_shape=(
            jax.ShapeDtypeStruct((part, tok), BF16),
            jax.ShapeDtypeStruct((part, tok), BF16),
            jax.ShapeDtypeStruct((part, depth), BF16),
        ),
        in_specs=[anywhere, anywhere, anywhere, smem, smem],
        out_specs=(vmem, vmem, vmem),
        scratch_shapes=[
            pltpu.VMEM((tok, depth), BF16), piece(part), block(BF16),
            block(F32), block(BF16), pltpu.VMEM((tok, part), BF16), row,
            block(BF16, pairs), pltpu.VMEM((pairs, 8, tok), F32), row,
            block(F32), block(F32), pltpu.VMEM((tok, tok), F32),
            pltpu.VMEM((pairs, tok, tok), F32),
            pltpu.VMEM((pairs, tok + TAIL, tok), BF16), pltpu.VMEM((pairs, tok + TAIL, tok), BF16),
            block(BF16, 4), block(BF16, 2), block(BF16), block(BF16), block(BF16), block(BF16),
            piece(half, F32), pltpu.VMEM((half, tok), BF16), piece(tok), piece(quarter), piece(quarter),
            piece(eighth), piece(eighth), piece(eighth, BF16, levels + 1), piece(eighth, BF16, levels),
            pltpu.VMEM((2, 8, tok), F32), pltpu.VMEM((2, 8, tok), F32),
            dma((4, CHUNKS)), dma((pairs, CHUNKS)), dma((pairs,)), dma((pairs,)), dma((4,)), dma((4,)),
            dma((11 + 2 * levels,)), dma((11 + 2 * levels,)), dma((3,)), dma((3,)), dma((3,)),
        ],
        compiler_params=pltpu.CompilerParams(
            collective_id=0, has_side_effects=True, vmem_limit_bytes=48 * 1024 * 1024
        ),
    )(*held, log_scale, logit_bias)
    return img_grad.T, txt_grad.T, weight_grad.T


def solution(mesh):
    in_specs = (P("dp", None), P(None, "rep"), P("dp", "rep"), P(), P())
    out_specs = (P("dp", "rep"), P("dp", "rep"), P(None, "rep"))
    body = functools.partial(shards, mesh.shape["dp"])
    return jax.shard_map(body, mesh=mesh, in_specs=in_specs, out_specs=out_specs, check_vma=False)
```

```python
import functools

import jax
import jax.numpy as jnp
from jax import lax
from jax.experimental import pallas as pl
from jax.experimental.pallas import tpu as pltpu
from jax.sharding import PartitionSpec as P

STEPS = 4
CHUNKS = 4
TAIL = 16
EPSILON = 1e-06
F32 = jnp.float32
BF16 = jnp.bfloat16
MESH = pl.DeviceIdType.MESH


def kernel(
    n, features_hbm, weight_hbm, text_hbm, log_scale, bias, img_out, txt_out, w_out,
    features, weight, text,
    img_hat, img_bf, img_rows, img_inv, span, squares, inverses, d_img, d_txt, dots,
    own_score, score_out, score_in, back, from_core, sum_two, sum_four, two_in, four_in,
    acc, core_grad, core_features, quarter_out, quarter_in, eighth_out, eighth_in,
    last_out, last_in, rows_out, rows_in,
    s_span, r_span, s_score, r_score, s_back, r_back, s_w, r_w, s_rows, r_rows, s_local,
):
    k = lax.axis_index("dp")
    x = lax.axis_index("rep")
    tok = features.shape[0]
    part = weight.shape[0]
    odd = lax.rem(k, 2)
    high = lax.rem(k // 2, 2)

    def bit(b):
        return lax.rem(k // b, 2)

    def flip(b):
        return k + b - 2 * b * bit(b)

    def at(offset):
        return (lax.rem(k + offset + n, n), x)

    core = (flip(1), x)
    across = (k, 1 - x)
    far = []
    b = 8
    while b < n:
        far.append(b)
        b *= 2

    def copy(src, dst, s, r, device):
        return pltpu.make_async_remote_copy(
            src_ref=src, dst_ref=dst, send_sem=s, recv_sem=r,
            device_id=device, device_id_type=MESH,
        )

    fetches = [
        pltpu.make_async_copy(src, dst, s_local.at[i])
        for i, (src, dst) in enumerate(
            ((weight_hbm, weight), (features_hbm, features), (text_hbm, text))
        )
    ]
    for fetch in fetches:
        fetch.start()
    barrier = pltpu.get_barrier_semaphore()
    friends = [across, core, at(2), at(-2), at(4), at(-4)] + [(flip(b), x) for b in far]
    for friend in friends:
        pl.semaphore_signal(barrier, inc=1, device_id=friend, device_id_type=MESH)
    pl.semaphore_wait(barrier, len(friends))

    size = part // CHUNKS

    def text_copy(source, target, c, device, i):
        piece = pl.ds(c * size, size)
        src = text_hbm if source is None else span.at[source]
        return copy(
            src.at[piece], span.at[target, piece], s_span.at[i, c], r_span.at[target, c], device
        )

    def arrived(s, c):
        piece = pl.ds(c * size, size)
        copy(
            span.at[s, piece], span.at[s, piece], s_span.at[0, c], r_span.at[s, c], core
        ).wait_recv()

    slot = 3 - 2 * odd
    own_four = [text_copy(None, 4, c, at(4), 0) for c in range(CHUNKS)]
    own_two = [text_copy(None, 2, c, at(2), 1) for c in range(CHUNKS)]
    pass_two = [text_copy(4, 2, c, at(-2), 1) for c in range(CHUNKS)]
    own_one = [text_copy(None, 1, c, core, 2) for c in range(CHUNKS)]
    pass_four = [text_copy(4, 3, c, core, 2) for c in range(CHUNKS)]
    share_two = [text_copy(2, slot, c, core, 3) for c in range(CHUNKS)]

    for c in range(CHUNKS):
        own_four[c].start()

        @pl.when(high == 0)
        def _():
            own_two[c].start()

        @pl.when(odd == 0)
        def _():
            own_one[c].start()

    core_features_copy = copy(features_hbm, core_features, s_rows.at[2], r_rows.at[2], core)

    def along(a, b):
        return lax.dot_general(a, b, (((1,), (1,)), ((), ())), preferred_element_type=F32)

    for fetch in fetches:
        fetch.wait()
    raw = along(weight[...], features[...])
    img_hat[...] = raw
    mine = jnp.sum(raw * raw, axis=0, keepdims=True)
    rows_out[0] = jnp.broadcast_to(mine, (8, tok))
    c = copy(rows_out.at[0], rows_in.at[0], s_rows.at[0], r_rows.at[0], across)
    c.start()
    t_wide = jnp.exp(jnp.full((1, tok), log_scale[0], F32))
    c.wait()
    inverse = lax.rsqrt(mine + rows_in[0, 0:1, :] + EPSILON)
    img_inv[...] = jnp.broadcast_to(inverse, (8, tok))
    hat = img_hat[...] * inverse
    img_hat[...] = hat
    img_bf[...] = hat.astype(BF16)
    img_rows[...] = jnp.transpose(img_bf[...])

    def text_of(s):
        return text[...] if isinstance(s, int) and s == 0 else span[s]

    def score_copy(s):
        return copy(score_out.at[s], score_in.at[s], s_score.at[s], r_score.at[s], across)

    def begin(s):
        block = text_of(s)
        score = jnp.dot(img_rows[...], block, preferred_element_type=F32)
        own_score[s] = score
        score_out[s, 0:tok, :] = score.astype(BF16)
        wide = block.astype(F32)
        square = jnp.sum(wide * wide, axis=0, keepdims=True)
        squares[s] = jnp.broadcast_to(square, (8, tok))
        top = square.astype(BF16).astype(F32)
        middle = (square - top).astype(BF16).astype(F32)
        low = square - top - middle
        row = lax.broadcasted_iota(jnp.int32, (TAIL, tok), 0)
        tail = jnp.where(row == 0, top, jnp.where(row == 1, middle, low))
        score_out[s, tok : tok + TAIL, :] = tail.astype(BF16)
        score_copy(s).start()

    def finish(s, first=False):
        score_copy(s).wait()
        tail = score_in[s, tok : tok + TAIL, :].astype(F32)
        square = squares[s, 0:1, :] + (tail[0:1] + tail[1:2] + tail[2:3])
        inverse = lax.rsqrt(square + EPSILON)
        if first:
            inverses[...] = jnp.broadcast_to(inverse, (8, tok))
        score = (own_score[s] + score_in[s, 0:tok, :].astype(F32)) * inverse
        g = jax.nn.sigmoid(t_wide * score + bias[0])
        if first:
            row = lax.broadcasted_iota(jnp.int32, (tok, tok), 0)
            col = lax.broadcasted_iota(jnp.int32, (tok, tok), 1)
            g = g - jnp.where(row == col, 1.0, 0.0)
        term = along(text_of(s), (g * inverse).astype(BF16))
        if first:
            d_img[...] = term
            dots[...] = g * score
        else:
            d_img[...] += term
            dots[...] += g * score
        return g.astype(BF16)

    def returned(g):
        return jnp.dot(img_bf[...], g, preferred_element_type=F32)

    def core_copy(i):
        return copy(back.at[2 * i], from_core.at[i], s_back.at[i], r_back.at[i], core)

    def choose(for_even, for_odd):
        return for_even + odd * (for_odd - for_even)

    oddf = odd.astype(F32)
    highf = high.astype(F32)
    send_two = copy(sum_two, two_in, s_back.at[2], r_back.at[2], (flip(2), x))
    send_four = copy(sum_four, four_in, s_back.at[3], r_back.at[3], at(-4))
    second, third, fifth = choose(4, 1), choose(3, 4), choose(1, 3)

    begin(0)
    core_features_copy.start()

    @pl.when(odd == 1)
    def _():
        for c in range(CHUNKS):
            arrived(1, c)

    @pl.when(odd == 0)
    def _():
        for c in range(CHUNKS):
            arrived(4, c)

            @pl.when(high == 1)
            def _():
                pass_two[c].start()

    begin(second)

    @pl.when(odd == 1)
    def _():
        for c in range(CHUNKS):
            arrived(4, c)
            pass_four[c].start()

            @pl.when(high == 1)
            def _():
                pass_two[c].start()

    d_txt[...] = returned(finish(0, True))

    @pl.when(odd == 0)
    def _():
        for c in range(CHUNKS):
            arrived(3, c)

    begin(third)
    back[second - 1] = returned(finish(second)).astype(BF16)

    @pl.when(odd == 1)
    def _():
        core_copy(0).start()

    for c in range(CHUNKS):
        arrived(2, c)
        share_two[c].start()
    begin(2)
    back[third - 1] = returned(finish(third)).astype(BF16)

    @pl.when(odd == 0)
    def _():
        core_copy(1).start()

    for c in range(CHUNKS):
        arrived(fifth, c)
    begin(fifth)
    back[1] = returned(finish(2)).astype(BF16)

    @pl.when(odd == 0)
    def _():
        sum_four[...] = back[3]

    @pl.when(odd == 1)
    def _():
        core_copy(1).wait_recv()
        sum_four[...] = (back[3].astype(F32) + from_core[1].astype(F32)).astype(BF16)

    @pl.when(high == 0)
    def _():
        send_four.start()

    last_g = finish(fifth)

    dot = jnp.sum(jnp.transpose(dots[...]), axis=0, keepdims=True)
    grad = (d_img[...] - img_hat[...] * dot) * (t_wide * img_inv[0:1, :])
    img_out[...] = grad.astype(BF16)

    half, quarter = part // 2, part // 4
    eighth = (quarter // 2 + 15) // 16 * 16
    rest = quarter - eighth
    depth = features.shape[1]
    cut = (depth // 2 + 127) // 128 * 128
    streams = (pl.ds(0, cut), pl.ds(cut, depth - cut))
    both = range(2)

    def rows(start, size):
        return pl.ds(pl.multiple_of(start, 16), size)

    swap = copy(
        img_out.at[rows((1 - odd) * half, half), :], core_grad, s_w.at[0], r_w.at[0], core
    )
    swap.start()
    back[fifth - 1] = returned(last_g).astype(BF16)

    @pl.when(odd == 0)
    def _():
        core_copy(0).start()

    @pl.when(odd == 1)
    def _():
        core_copy(1).start()

    first_b, second_b = 2 + 2 * odd, 4 - 2 * odd
    first_bit = high * (1 - odd) + bit(4) * odd
    second_bit = high * odd + bit(4) * (1 - odd)
    first_peer = (k + first_b - 2 * first_b * first_bit, x)
    second_peer = (k + second_b - 2 * second_b * second_bit, x)
    keep = first_bit * quarter
    mine_at = keep + second_bit * rest
    base = odd * half + keep

    def stage(i, u, src, dst, device):
        lanes = streams[u]
        return copy(
            src.at[:, lanes], dst.at[:, lanes], s_w.at[1 + 2 * i + u], r_w.at[1 + 2 * i + u], device
        )

    acc[...] = jnp.dot(img_out[rows(odd * half, half), :], features[...], preferred_element_type=F32)
    swap.wait()
    core_features_copy.wait()
    two, three = [], []
    for u in both:
        lanes = streams[u]
        acc[:, lanes] += jnp.dot(
            core_grad[...], core_features[:, lanes], preferred_element_type=F32
        )
        quarter_out[:, lanes] = acc[rows((1 - first_bit) * quarter, quarter), lanes].astype(BF16)
        two.append(stage(0, u, quarter_out, quarter_in, first_peer))
        two[u].start()

    for u in both:
        lanes = streams[u]
        two[u].wait()
        acc[rows(keep, quarter), lanes] += quarter_in[:, lanes].astype(F32)
        eighth_out[:, lanes] = acc[
            rows(keep + (1 - second_bit) * rest, eighth), lanes
        ].astype(BF16)
        three.append(stage(1, u, eighth_out, eighth_in, second_peer))
        three[u].start()

    core_copy(0).wait_recv()

    @pl.when(odd == 0)
    def _():
        core_copy(1).wait_recv()

    sum_two[...] = (back[1].astype(F32) + from_core[1 - odd].astype(F32)).astype(BF16)
    send_two.start()

    def exchange(i, u):
        return stage(5 + i, u, last_out.at[i], last_in.at[i], (flip(far[i]), x))

    for u in both:
        lanes = streams[u]
        three[u].wait()
        total = acc[rows(mine_at, eighth), lanes] + eighth_in[:, lanes].astype(F32)
        last_out[0, :, lanes] = total.astype(BF16)
        if far:
            exchange(0, u).start()

    def spread(i, u, start, size, device):
        piece = w_out.at[rows(start, size), streams[u]]
        return copy(piece, piece, s_w.at[1 + 2 * i + u], r_w.at[1 + 2 * i + u], device)

    for i in range(len(far)):
        for u in both:
            lanes = streams[u]
            exchange(i, u).wait()
            total = last_out[i, :, lanes].astype(F32) + last_in[i, :, lanes].astype(F32)
            last_out[i + 1, :, lanes] = total.astype(BF16)
            if i + 1 < len(far):
                exchange(i + 1, u).start()

    for u in both:
        lanes = streams[u]

        @pl.when(second_bit == 0)
        def _():
            w_out[rows(base, eighth), lanes] = last_out[len(far), :, lanes]
            spread(2, u, base, eighth, second_peer).start()

        @pl.when(second_bit == 1)
        def _():
            w_out[rows(base + eighth, rest), lanes] = last_out[len(far), eighth - rest :, lanes]
            spread(2, u, base + eighth, rest, second_peer).start()

    send_two.wait()

    @pl.when(high == 1)
    def _():
        sum_four[...] = (
            back[3].astype(F32) + from_core[1].astype(F32) * oddf + two_in[...].astype(F32)
        ).astype(BF16)
        send_four.start()

    for u in both:

        @pl.when(second_bit == 0)
        def _():
            spread(2, u, base, eighth, second_peer).wait_send()
            spread(2, u, base + eighth, rest, second_peer).wait_recv()

        @pl.when(second_bit == 1)
        def _():
            spread(2, u, base + eighth, rest, second_peer).wait_send()
            spread(2, u, base, eighth, second_peer).wait_recv()

        spread(3, u, base, quarter, first_peer).start()

    for u in both:
        spread(3, u, odd * half + (1 - first_bit) * quarter, quarter, first_peer).wait_recv()
        spread(4, u, odd * half, half, core).start()

    send_four.wait()
    even = 1.0 - oddf
    grad = (
        d_txt[...] + four_in[...].astype(F32) + from_core[0].astype(F32) * even
        + two_in[...].astype(F32) * (1.0 - highf)
    )
    d_txt[...] = grad
    hat = text[...].astype(F32) * inverses[0:1, :]
    dot = jnp.sum(hat * grad, axis=0, keepdims=True)
    rows_out[1] = jnp.broadcast_to(dot, (8, tok))
    cd = copy(rows_out.at[1], rows_in.at[1], s_rows.at[1], r_rows.at[1], across)
    cd.start()
    cd.wait()
    dot = dot + rows_in[1, 0:1, :]
    inverse = inverses[0:1, :]
    hat = text[...].astype(F32) * inverse
    txt_out[...] = ((d_txt[...] - hat * dot) * (t_wide * inverse)).astype(BF16)

    for u in both:
        spread(4, u, (1 - odd) * half, half, core).wait_recv()
        spread(3, u, base, quarter, first_peer).wait_send()
        spread(4, u, odd * half, half, core).wait_send()
    core_copy(0).wait_send()
    core_copy(1).wait_send()
    for c in range(CHUNKS):
        own_four[c].wait_send()
        share_two[c].wait_send()

        @pl.when(high == 0)
        def _():
            own_two[c].wait_send()

        @pl.when(high == 1)
        def _():
            pass_two[c].wait_send()

        @pl.when(odd == 0)
        def _():
            own_one[c].wait_send()

        @pl.when(odd == 1)
        def _():
            pass_four[c].wait_send()


def shards(n, features, img_weight, text_embed, log_scale, logit_bias):
    tok, depth = features.shape
    part = img_weight.shape[1]
    vmem = pl.BlockSpec(memory_space=pltpu.VMEM)
    anywhere = pl.BlockSpec(memory_space=pltpu.HBM)
    smem = pl.BlockSpec(memory_space=pltpu.SMEM)

    def block(dtype, *lead):
        return pltpu.VMEM((*lead, part, tok), dtype)

    def piece(size, dtype=BF16, *lead):
        return pltpu.VMEM((*lead, size, depth), dtype)

    levels = 1
    while 8 << levels < n:
        levels += 1
    dma = pltpu.SemaphoreType.DMA
    pairs = STEPS + 1
    half, quarter = part // 2, part // 4
    eighth = (quarter // 2 + 15) // 16 * 16
    row = pltpu.VMEM((8, tok), F32)
    held = [
        pltpu.with_memory_space_constraint(a, pltpu.HBM)
        for a in (features, img_weight.T, text_embed.T)
    ]
    img_grad, txt_grad, weight_grad = pl.pallas_call(
        functools.partial(kernel, n),
        out_shape=(
            jax.ShapeDtypeStruct((part, tok), BF16),
            jax.ShapeDtypeStruct((part, tok), BF16),
            jax.ShapeDtypeStruct((part, depth), BF16),
        ),
        in_specs=[anywhere, anywhere, anywhere, smem, smem],
        out_specs=(vmem, vmem, vmem),
        scratch_shapes=[
            pltpu.VMEM((tok, depth), BF16), piece(part), block(BF16),
            block(F32), block(BF16), pltpu.VMEM((tok, part), BF16), row,
            block(BF16, pairs), pltpu.VMEM((pairs, 8, tok), F32), row,
            block(F32), block(F32), pltpu.VMEM((tok, tok), F32),
            pltpu.VMEM((pairs, tok, tok), F32),
            pltpu.VMEM((pairs, tok + TAIL, tok), BF16), pltpu.VMEM((pairs, tok + TAIL, tok), BF16),
            block(BF16, 4), block(BF16, 2), block(BF16), block(BF16), block(BF16), block(BF16),
            piece(half, F32), pltpu.VMEM((half, tok), BF16), piece(tok), piece(quarter), piece(quarter),
            piece(eighth), piece(eighth), piece(eighth, BF16, levels + 1), piece(eighth, BF16, levels),
            pltpu.VMEM((2, 8, tok), F32), pltpu.VMEM((2, 8, tok), F32),
            dma((4, CHUNKS)), dma((pairs, CHUNKS)), dma((pairs,)), dma((pairs,)), dma((4,)), dma((4,)),
            dma((11 + 2 * levels,)), dma((11 + 2 * levels,)), dma((3,)), dma((3,)), dma((3,)),
        ],
        compiler_params=pltpu.CompilerParams(
            collective_id=0, has_side_effects=True, vmem_limit_bytes=48 * 1024 * 1024
        ),
    )(*held, log_scale, logit_bias)
    return img_grad.T, txt_grad.T, weight_grad.T


def solution(mesh):
    in_specs = (P("dp", None), P(None, "rep"), P("dp", "rep"), P(), P())
    out_specs = (P("dp", "rep"), P("dp", "rep"), P(None, "rep"))
    body = functools.partial(shards, mesh.shape["dp"])
    return jax.shard_map(body, mesh=mesh, in_specs=in_specs, out_specs=out_specs, check_vma=False)
```
